32 devices in a mesh: row: 8 (over z, x), col: 4 (over y, core).
Axes of the slice: x: 2, y: 2, z: 4, core: 2. Of those that a mesh axis runs over, the one named last changes fastest.
Arguments:
- x_rhs: bfloat16 [16, 1024, 1024], P('col', 'row'), may hold values from -6 to 6
- panel_u: bfloat16 [16, 1024, 256], P('row', 'col'), may hold values from -0.1875 to 0.1875
- panel_v: bfloat16 [16, 1024, 256], P('row', 'col'), may hold values from -0.1875 to 0.1875
- panel_rank: int32 [16], replicated, may hold values from 32 to 256, as said below
- tile_p: bfloat16 [16, 16, 1024, 256], P('row', 'col'), may hold values from -0.09375 to 0.09375
- tile_q: bfloat16 [16, 16, 1024, 256], P('row', 'col'), may hold values from -0.1875 to 0.1875
- tile_rank: int32 [16, 16], P('row', 'col'), may hold values from 32 to 256, as said below
Outputs:
- kriged: bfloat16 [16, 1024, 1024], P('row', None, 'col')
The draws below stay inside these ranges and needn't reach their ends.
Inputs may be any that keep to these rules, and one draw needn't show every extreme that they name: `panel_rank`: each panel tile's rank; the columns at or beyond it carry no part of the tile. `tile_rank`: each trailing tile's rank; the columns at or beyond it carry no part of the tile.
All inputs are finite; a program needn't handle non-finite values.
Results may differ from the reference program's by a relative error of at most 0.018.
Values may be sent and summed in bfloat16 or wider, within the bound.
A program may use at most 64 MiB of HBM per device.

```python
import jax
import jax.numpy as jnp
from jax import lax

B = 1024
R = 256
NRHS = 1024
NT = 16


def rank_values(key, shape):
    level_draw = jax.random.randint(jax.random.fold_in(key, 11), shape, 0, 16)
    low_rank = R // 8
    flat_ranks = (low_rank + level_draw * level_draw * (R - low_rank) // 225).reshape(-1)
    flat_ranks = jnp.minimum(flat_ranks, R).astype(jnp.int32)
    count_all = flat_ranks.shape[0]
    top_spot = jax.random.randint(jax.random.fold_in(key, 12), (), 0, count_all)
    step_away = jax.random.randint(jax.random.fold_in(key, 13), (), 1, count_all)
    bottom_spot = (top_spot + step_away) % count_all
    flat_ranks = flat_ranks.at[top_spot].set(R)
    flat_ranks = flat_ranks.at[bottom_spot].set(low_rank)
    return flat_ranks.reshape(shape).astype(jnp.int32)


def draw_panel_rank(key, part):
    return rank_values(jax.random.fold_in(key, 101), (NT,))


def draw_tile_rank(key, part):
    return rank_values(jax.random.fold_in(key, 202), (NT, NT))


def level_of(stream_key, extent, pieces, smallest, high):
    loudness = 1.0
    for position, shards_of in pieces:
        steps = jax.random.uniform(jax.random.fold_in(jax.random.fold_in(stream_key, 6), position), (shards_of,), jnp.float32, smallest / len(pieces), high / len(pieces))
        loudness = loudness * jnp.repeat(jnp.exp(steps), extent[position] // shards_of).reshape((-1,) + (1,) * (len(extent) - 1 - position))
    return loudness


def normal_values(own_key, shape, deviation, reach, shards=(), kind=jnp.bfloat16):
    array = jax.random.normal(own_key, shape, jnp.float32) * deviation
    if len(shards) > 0:
        array = level_of(own_key, shape, shards, -0.22, 0.18) * array
    return jnp.clip(array, min=-reach, max=reach).astype(kind)


def setup_inputs(seed: int = 0) -> dict:
    keys = jax.random.split(jax.random.key(seed), 8)
    return {
        "x_rhs": normal_values(keys[0], (NT, B, NRHS), 1.0, 6.0, ((0, 4), (1, 8))),
        "panel_u": normal_values(keys[1], (NT, B, R), B ** -0.5, 0.1875, ((0, 8), (1, 4))),
        "panel_v": normal_values(keys[2], (NT, B, R), (4 * R) ** -0.5, 0.1875, ((0, 8), (1, 4))),
        "panel_rank": draw_panel_rank(jax.random.fold_in(keys[7], 71), 0),
        "tile_p": normal_values(keys[4], (NT, NT, B, R), (R * NT) ** -0.5, 0.09375, ((0, 8), (1, 4))),
        "tile_q": normal_values(keys[5], (NT, NT, B, R), B ** -0.5, 0.1875, ((0, 8), (1, 4))),
        "tile_rank": draw_tile_rank(jax.random.fold_in(keys[7], 71), 0),
    }


def reference(x_rhs, panel_u, panel_v, panel_rank, tile_p, tile_q, tile_rank):
    exact = lax.Precision.HIGHEST
    rank_slot = jnp.arange(R, dtype=jnp.int32)
    rhs_wide = x_rhs.astype(jnp.float32)
    u_wide = panel_u.astype(jnp.float32)
    v_wide = panel_v.astype(jnp.float32)
    panel_mask = rank_slot[None, :, None] < panel_rank[:, None, None]
    panel_proj = jnp.einsum("jbr,jbn->jrn", u_wide, rhs_wide, precision=exact)
    panel_proj = jnp.where(panel_mask, panel_proj, jnp.float32(0.0)).astype(jnp.bfloat16)
    sweep = jnp.einsum("jbr,jrn->bn", v_wide, panel_proj.astype(jnp.float32), precision=exact)
    back_proj = jnp.einsum("ibr,bn->irn", v_wide, sweep, precision=exact)
    back_proj = jnp.where(panel_mask, back_proj, jnp.float32(0.0))
    correction = jnp.einsum("ibr,irn->ibn", u_wide, back_proj, precision=exact)

    def one_row(packed):
        p_row, q_row, rank_row = packed
        tile_proj = jnp.einsum("jbr,jbn->jrn", q_row.astype(jnp.float32), rhs_wide, precision=exact)
        tile_mask = rank_slot[None, :, None] < rank_row[:, None, None]
        tile_proj = jnp.where(tile_mask, tile_proj, jnp.float32(0.0)).astype(jnp.bfloat16)
        return jnp.einsum("jbr,jrn->bn", p_row.astype(jnp.float32), tile_proj.astype(jnp.float32), precision=exact)

    base_sum = lax.map(one_row, (tile_p, tile_q, tile_rank))
    return (base_sum - correction).astype(jnp.bfloat16)
```

```python
import functools

import jax
import jax.numpy as jnp
from jax import lax
from jax.experimental import pallas as pl
from jax.experimental.pallas import tpu as pltpu
from jax.sharding import PartitionSpec as P

BF16 = jnp.bfloat16
F32 = jnp.float32
MESH = pl.DeviceIdType.MESH
UP, DOWN, ACROSS = 0, 1, 2


def plain(x_rhs, panel_u, panel_v, panel_rank, tile_p, tile_q, tile_rank):
    exact = lax.Precision.HIGHEST
    row_at = lax.axis_index("row")
    col_at = lax.axis_index("col")
    t_rows = tile_p.shape[0]
    t_cols = tile_p.shape[1]
    rank_cap = tile_p.shape[3]
    gathered = lax.all_gather(x_rhs, "row", axis=1, tiled=True)
    full_u, full_v = (
        lax.all_gather(panel_u, "col", axis=1, tiled=True),
        lax.all_gather(panel_v, "col", axis=1, tiled=True),
    )
    tile_slot = lax.broadcasted_iota(jnp.int32, (1, 1, rank_cap, 1), 2)
    tile_proj = jnp.einsum("ijbr,jbn->ijrn", tile_q, gathered, preferred_element_type=jnp.float32)
    tile_proj = jnp.where(tile_slot < tile_rank[:, :, None, None], tile_proj, 0.0).astype(
        jnp.bfloat16
    )
    base_sum = jnp.einsum("ijbr,ijrn->ibn", tile_p, tile_proj, preferred_element_type=jnp.float32)
    rank_slot = lax.broadcasted_iota(jnp.int32, (1, rank_cap, 1), 1)
    row_rank = lax.dynamic_slice_in_dim(panel_rank, row_at * t_rows, t_rows)
    row_keep = rank_slot < row_rank[:, None, None]
    u_wide = full_u.astype(jnp.float32)
    tile_ids = row_at * t_rows + jnp.arange(t_rows, dtype=jnp.int32)
    inside = tile_ids // t_cols == col_at
    where_rhs = jnp.clip(tile_ids - col_at * t_cols, 0, t_cols - 1)
    picked = jnp.take(gathered, where_rhs, axis=0)
    keep = jnp.logical_and(inside[:, None, None], row_keep)
    panel_proj = jnp.einsum("jbr,jbn->jrn", full_u, picked, preferred_element_type=jnp.float32)
    panel_proj = jnp.where(keep, panel_proj, 0.0).astype(jnp.bfloat16)
    sweep_part = jnp.einsum("jbr,jrn->bn", full_v, panel_proj, preferred_element_type=jnp.float32)
    sweep_share = lax.psum_scatter(
        sweep_part.astype(jnp.bfloat16), "col", scatter_dimension=1, tiled=True
    )
    sweep = lax.psum(sweep_share, "row").astype(jnp.float32)
    back_proj = jnp.einsum("ibr,bn->irn", full_v.astype(jnp.float32), sweep, precision=exact)
    back_proj = jnp.where(row_keep, back_proj, 0.0)
    late_term = jnp.einsum("ibr,irn->ibn", u_wide, back_proj, precision=exact)
    summed = lax.psum_scatter(
        base_sum.astype(jnp.bfloat16), "col", scatter_dimension=2, tiled=True
    ).astype(jnp.float32)
    return (summed - late_term).astype(jnp.bfloat16)


def dot(a, b):
    return jnp.dot(a, b, preferred_element_type=F32)


def kernel(
    n_row, n_col,
    tile_rank, panel_rank, x_in, u_in, v_in, p_in, q_in,
    out,
    xg, pv, qv, qt, ug, vg, ut, vt, acc, sweep_acc, sbuf, rbuf, swb, swr, swg,
    x_send, x_recv, uv_send, uv_recv, b_send, b_recv, sw_send, sw_recv, g_send, g_recv, local,
):
    t_rows, t_cols, order, rank_cap = pv.shape
    x_rows = xg.shape[3]
    width = xg.shape[4]
    u_rows = ug.shape[2]
    steps = n_col
    line = n_row // 2
    row = lax.axis_index("row")
    col = lax.axis_index("col")
    z, x = row // 2, row % 2
    inside = (row * t_rows) // t_cols == col
    first = lax.rem(row * t_rows, t_cols)

    def owner(s):
        return lax.rem(col + 1 + s, n_col)

    def x_local(s):
        at = pl.multiple_of(owner(s) * width, width)
        return pltpu.make_async_copy(x_in.at[:, :, pl.ds(at, width)], xg.at[s, row], local.at[s])

    q_local = pltpu.make_async_copy(q_in, qv, local.at[steps])
    p_local = pltpu.make_async_copy(p_in, pv, local.at[steps + 1])
    u_local = pltpu.make_async_copy(u_in, ug.at[col], local.at[steps + 2])
    v_local = pltpu.make_async_copy(v_in, vg.at[col], local.at[steps + 3])
    x_local(0).start()
    u_local.start()
    v_local.start()
    for s in range(1, steps):
        x_local(s).start()
    q_local.start()
    p_local.start()

    barrier = pltpu.get_barrier_semaphore()

    @pl.loop(0, n_row * n_col)
    def _(k):
        @pl.when(k != row * n_col + col)
        def _():
            pl.semaphore_signal(
                barrier, inc=1, device_id=(k // n_col, lax.rem(k, n_col)), device_id_type=MESH
            )

    pl.semaphore_wait(barrier, n_row * n_col - 1)

    def x_copy(s, k, way):
        target = {UP: row + 2, DOWN: row - 2, ACROSS: row + 1 - 2 * x}[way]
        return pltpu.make_async_remote_copy(
            src_ref=xg.at[s, k], dst_ref=xg.at[s, k],
            send_sem=x_send.at[s, k, way], recv_sem=x_recv.at[s, k],
            device_id=(target, col), device_id_type=MESH,
        )

    def own_sends(s):
        x_local(s).wait()
        x_copy(s, row, ACROSS).start()

        @pl.when(z + 1 < line)
        def _():
            x_copy(s, row, UP).start()

        @pl.when(z > 0)
        def _():
            x_copy(s, row, DOWN).start()

    def forward(s, d):
        @pl.when(z - d >= 0)
        def _():
            k = row - 2 * d
            x_copy(s, k, ACROSS).wait_recv()
            x_copy(s, k, ACROSS).start()

            @pl.when(z + 1 < line)
            def _():
                x_copy(s, k, UP).start()

        @pl.when(z + d < line)
        def _():
            k = row + 2 * d
            x_copy(s, k, ACROSS).wait_recv()
            x_copy(s, k, ACROSS).start()

            @pl.when(z > 0)
            def _():
                x_copy(s, k, DOWN).start()

    def uv_copy(which, d, slot):
        ref = (ug, vg)[which]
        return pltpu.make_async_remote_copy(
            src_ref=ref.at[slot], dst_ref=ref.at[slot],
            send_sem=uv_send.at[which, d], recv_sem=uv_recv.at[which, d],
            device_id=(row, lax.rem(col + d, n_col)), device_id_type=MESH,
        )

    own_sends(0)
    u_local.wait()
    v_local.wait()
    for d in range(1, n_col):
        uv_copy(0, d, col).start()
        uv_copy(1, d, col).start()
    own_sends(1)

    q_local.wait()

    @pl.loop(0, t_rows * t_cols)
    def _(k):
        i, j = k // t_cols, lax.rem(k, t_cols)
        keep = lax.broadcasted_iota(jnp.int32, (rank_cap, u_rows), 0) < tile_rank[i, j]
        for b in range(order // u_rows):
            at = pl.ds(b * u_rows, u_rows)
            qt[i, j, :, at] = jnp.where(keep, qv[i, j, at, :].T, jnp.zeros((), BF16))

    p_local.wait()
    for d in range(1, n_col):
        slot = lax.rem(col + n_col - d, n_col)
        uv_copy(0, d, slot).wait_recv()
        uv_copy(1, d, slot).wait_recv()

    @pl.loop(0, t_rows)
    def _(i):
        keep = (
            lax.broadcasted_iota(jnp.int32, (rank_cap, u_rows), 0) < panel_rank[row * t_rows + i]
        )
        for b in range(n_col):
            at = pl.ds(b * u_rows, u_rows)
            ut[i, :, at] = jnp.where(keep, ug[b, i].T, jnp.zeros((), BF16))
            vt[i, :, at] = jnp.where(keep, vg[b, i].T, jnp.zeros((), BF16))

    def b_copy(s):
        return pltpu.make_async_remote_copy(
            src_ref=sbuf.at[s], dst_ref=rbuf.at[s],
            send_sem=b_send.at[s], recv_sem=b_recv.at[s],
            device_id=(row, owner(s)), device_id_type=MESH,
        )

    def sw_copy(s, k):
        return pltpu.make_async_remote_copy(
            src_ref=swb.at[s, k], dst_ref=swr.at[row],
            send_sem=sw_send.at[s, k], recv_sem=sw_recv.at[row],
            device_id=(k, owner(s)), device_id_type=MESH,
        )

    def compute(s):
        for k in range(line):
            x_copy(s, 2 * k + 1 - x, ACROSS).wait_recv()

        @pl.when(inside)
        def _():
            for i in range(t_rows):
                block = xg[s, :, first + i].reshape(order, width)
                proj = dot(ut[i], block).astype(BF16)
                term = dot(vg[:, i].reshape(order, rank_cap), proj)
                if i == 0:
                    sweep_acc[...] = term
                else:
                    sweep_acc[...] += term
            swb[s] = sweep_acc[...].astype(BF16).reshape(n_row, x_rows, width)

            @pl.loop(0, n_row)
            def _(k):
                mine = jnp.logical_and(k == row, s == steps - 1)

                @pl.when(mine)
                def _():
                    swr[row] = swb[s, row]

                @pl.when(jnp.logical_not(mine))
                def _():
                    sw_copy(s, k).start()

        @pl.loop(0, t_rows)
        def _(i):
            total = None
            for j in range(t_cols):
                proj = dot(qt[i, j], xg[s, :, j].reshape(order, width)).astype(BF16)
                term = dot(pv[i, j], proj)
                total = term if total is None else total + term

            acc[i] = total

            @pl.when(s < steps - 1)
            def _():
                sbuf[s, i] = acc[i].astype(BF16)

        @pl.when(s < steps - 1)
        def _():
            b_copy(s).start()

    @pl.loop(0, steps + 1)
    def _(s):
        @pl.when(s < steps)
        def _():
            forward(s, 1)

        @pl.when(s + 2 < steps)
        def _():
            own_sends(s + 2)

        @pl.when(s > 0)
        def _():
            compute(s - 1)

        @pl.when(s < steps)
        def _():
            for d in range(2, line):
                forward(s, d)

    for k in range(n_row):
        @pl.when(jnp.logical_not(jnp.logical_and(inside, k == row)))
        def _():
            pltpu.make_async_remote_copy(
                src_ref=swr.at[k], dst_ref=swr.at[k],
                send_sem=sw_send.at[0, 0], recv_sem=sw_recv.at[k],
                device_id=(row, col), device_id_type=MESH,
            ).wait_recv()

    swg[row] = functools.reduce(lambda a, k: a + swr[k].astype(F32), range(1, n_row), swr[0].astype(F32)).astype(BF16)

    def g_copy(d, slot):
        return pltpu.make_async_remote_copy(
            src_ref=swg.at[slot], dst_ref=swg.at[slot],
            send_sem=g_send.at[d], recv_sem=g_recv.at[d],
            device_id=(lax.rem(row + d, n_row), col), device_id_type=MESH,
        )

    for d in range(1, n_row):
        g_copy(d, row).start()
    for s in range(steps - 1):
        b_copy(s).wait_recv()

    @pl.loop(0, t_rows)
    def _(i):
        total = acc[i]
        for s in range(steps - 1):
            total = total + rbuf[s, i].astype(F32)
        acc[i] = total

    for d in range(1, n_row):
        g_copy(d, lax.rem(row + n_row - d, n_row)).wait_recv()

    @pl.loop(0, t_rows)
    def _(i):
        back = dot(vt[i], swg[...].reshape(order, width)).astype(BF16)
        late = dot(ug[:, i].reshape(order, rank_cap), back)
        out[i] = (acc[i] - late).astype(BF16)

    @pl.loop(0, steps)
    def _(s):
        for m in range(line):
            k = 2 * m + x
            x_copy(s, k, ACROSS).wait_send()

            @pl.when(jnp.logical_and(m <= z, z + 1 < line))
            def _():
                x_copy(s, k, UP).wait_send()

            @pl.when(jnp.logical_and(m >= z, z > 0))
            def _():
                x_copy(s, k, DOWN).wait_send()

        @pl.when(s < steps - 1)
        def _():
            b_copy(s).wait_send()

        @pl.when(inside)
        def _():
            @pl.loop(0, n_row)
            def _(k):
                @pl.when(jnp.logical_not(jnp.logical_and(k == row, s == steps - 1)))
                def _():
                    sw_copy(s, k).wait_send()

    for d in range(1, n_col):
        uv_copy(0, d, col).wait_send()
        uv_copy(1, d, col).wait_send()
    for d in range(1, n_row):
        g_copy(d, row).wait_send()


def shards(n_row, n_col, x_rhs, panel_u, panel_v, panel_rank, tile_p, tile_q, tile_rank):
    t_rows, t_cols, order, rank_cap = tile_p.shape
    x_rows, n_rhs = x_rhs.shape[1:]
    u_rows = panel_u.shape[1]
    width = n_rhs // n_col
    fits = (
        width % 128 == 0
        and x_rows % 16 == 0
        and u_rows % 128 == 0
        and n_row % 2 == 0
        and n_row > 2
        and n_col > 1
        and t_cols % t_rows == 0
        and n_rhs % n_col == 0
    )
    if not fits:
        return plain(x_rhs, panel_u, panel_v, panel_rank, tile_p, tile_q, tile_rank)
    dma = pltpu.SemaphoreType.DMA
    flops = 4 * order * rank_cap * n_rhs * t_rows * (t_cols + 1)
    return pl.pallas_call(
        functools.partial(kernel, n_row, n_col),
        out_shape=jax.ShapeDtypeStruct((t_rows, order, width), BF16),
        in_specs=[pl.BlockSpec(memory_space=pltpu.SMEM)] * 2
        + [pl.BlockSpec(memory_space=pl.ANY)] * 5,
        out_specs=pl.BlockSpec(memory_space=pltpu.VMEM),
        scratch_shapes=[
            pltpu.VMEM((n_col, n_row, t_cols, x_rows, width), BF16),
            pltpu.VMEM(tile_p.shape, BF16),
            pltpu.VMEM(tile_q.shape, BF16),
            pltpu.VMEM((t_rows, t_cols, rank_cap, order), BF16),
            pltpu.VMEM((n_col, t_rows, u_rows, rank_cap), BF16),
            pltpu.VMEM((n_col, t_rows, u_rows, rank_cap), BF16),
            pltpu.VMEM((t_rows, rank_cap, order), BF16),
            pltpu.VMEM((t_rows, rank_cap, order), BF16),
            pltpu.VMEM((t_rows, order, width), F32),
            pltpu.VMEM((order, width), F32),
            pltpu.VMEM((n_col - 1, t_rows, order, width), BF16),
            pltpu.VMEM((n_col - 1, t_rows, order, width), BF16),
            pltpu.VMEM((n_col, n_row, x_rows, width), BF16),
            pltpu.VMEM((n_row, x_rows, width), BF16),
            pltpu.VMEM((n_row, x_rows, width), BF16),
            dma((n_col, n_row, 3)),
            dma((n_col, n_row)),
            dma((2, n_col)),
            dma((2, n_col)),
            dma((n_col,)),
            dma((n_col,)),
            dma((n_col, n_row)),
            dma((n_row,)),
            dma((n_row,)),
            dma((n_row,)),
            dma((n_col + 4,)),
        ],
        compiler_params=pltpu.CompilerParams(
            collective_id=0, has_side_effects=True, vmem_limit_bytes=56 * 2**20
        ),
        cost_estimate=pl.CostEstimate(flops=flops, bytes_accessed=20 * 2**20, transcendentals=0),
    )(tile_rank, panel_rank, x_rhs, panel_u, panel_v, tile_p, tile_q)


def solution(mesh):
    return jax.shard_map(
        functools.partial(shards, mesh.shape["row"], mesh.shape["col"]),
        mesh=mesh,
        in_specs=(
            P("col", "row", None),
            P("row", "col", None),
            P("row", "col", None),
            P(),
            P("row", "col", None, None),
            P("row", "col", None, None),
            P("row", "col"),
        ),
        out_specs=P("row", None, "col"),
        check_vma=False,
    )
```

```python
import functools

import jax
import jax.numpy as jnp
from jax import lax
from jax.experimental import pallas as pl
from jax.experimental.pallas import tpu as pltpu
from jax.sharding import PartitionSpec as P

BF16 = jnp.bfloat16
F32 = jnp.float32
MESH = pl.DeviceIdType.MESH
UP, DOWN, ACROSS = 0, 1, 2


def plain(x_rhs, panel_u, panel_v, panel_rank, tile_p, tile_q, tile_rank):
    exact = lax.Precision.HIGHEST
    row_at = lax.axis_index("row")
    col_at = lax.axis_index("col")
    t_rows = tile_p.shape[0]
    t_cols = tile_p.shape[1]
    rank_cap = tile_p.shape[3]
    gathered = lax.all_gather(x_rhs, "row", axis=1, tiled=True)
    full_u, full_v = (
        lax.all_gather(panel_u, "col", axis=1, tiled=True),
        lax.all_gather(panel_v, "col", axis=1, tiled=True),
    )
    tile_slot = lax.broadcasted_iota(jnp.int32, (1, 1, rank_cap, 1), 2)
    tile_proj = jnp.einsum("ijbr,jbn->ijrn", tile_q, gathered, preferred_element_type=jnp.float32)
    tile_proj = jnp.where(tile_slot < tile_rank[:, :, None, None], tile_proj, 0.0).astype(
        jnp.bfloat16
    )
    base_sum = jnp.einsum("ijbr,ijrn->ibn", tile_p, tile_proj, preferred_element_type=jnp.float32)
    rank_slot = lax.broadcasted_iota(jnp.int32, (1, rank_cap, 1), 1)
    row_rank = lax.dynamic_slice_in_dim(panel_rank, row_at * t_rows, t_rows)
    row_keep = rank_slot < row_rank[:, None, None]
    u_wide = full_u.astype(jnp.float32)
    tile_ids = row_at * t_rows + jnp.arange(t_rows, dtype=jnp.int32)
    inside = tile_ids // t_cols == col_at
    where_rhs = jnp.clip(tile_ids - col_at * t_cols, 0, t_cols - 1)
    picked = jnp.take(gathered, where_rhs, axis=0)
    keep = jnp.logical_and(inside[:, None, None], row_keep)
    panel_proj = jnp.einsum("jbr,jbn->jrn", full_u, picked, preferred_element_type=jnp.float32)
    panel_proj = jnp.where(keep, panel_proj, 0.0).astype(jnp.bfloat16)
    sweep_part = jnp.einsum("jbr,jrn->bn", full_v, panel_proj, preferred_element_type=jnp.float32)
    sweep_share = lax.psum_scatter(
        sweep_part.astype(jnp.bfloat16), "col", scatter_dimension=1, tiled=True
    )
    sweep = lax.psum(sweep_share, "row").astype(jnp.float32)
    back_proj = jnp.einsum("ibr,bn->irn", full_v.astype(jnp.float32), sweep, precision=exact)
    back_proj = jnp.where(row_keep, back_proj, 0.0)
    late_term = jnp.einsum("ibr,irn->ibn", u_wide, back_proj, precision=exact)
    summed = lax.psum_scatter(
        base_sum.astype(jnp.bfloat16), "col", scatter_dimension=2, tiled=True
    ).astype(jnp.float32)
    return (summed - late_term).astype(jnp.bfloat16)


def dot(a, b):
    return jnp.dot(a, b, preferred_element_type=F32)


def kernel(
    n_row, n_col,
    tile_rank, panel_rank, x_in, u_in, v_in, p_in, q_in,
    out,
    xg, pv, qv, qt, ug, vg, ut, vt, acc, sweep_acc, sbuf, rbuf, swb, swr, swg,
    x_send, x_recv, h_send, h_recv, uv_send, uv_recv, b_send, b_recv, sw_send, sw_recv, g_send, g_recv, local,
):
    t_rows, t_cols, order, rank_cap = pv.shape
    x_rows = xg.shape[3]
    width = xg.shape[4]
    u_rows = ug.shape[2]
    subs = swr.shape[0]
    steps = n_col * subs
    away = steps - subs
    ahead = 3
    half = t_cols // 2
    line = n_row // 2
    row = lax.axis_index("row")
    col = lax.axis_index("col")
    z, x = row // 2, row % 2
    mate = row + 1 - 2 * x
    odd = z % 2 == 1
    twin = row + 2 - 4 * (z % 2)
    inside = (row * t_rows) // t_cols == col
    first = lax.rem(row * t_rows, t_cols)

    def owner(s):
        return lax.rem(col + 1 + s // subs, n_col)

    def x_local(s):
        at = pl.multiple_of((owner(s) * subs + lax.rem(s, subs)) * width, width)
        return pltpu.make_async_copy(x_in.at[:, :, pl.ds(at, width)], xg.at[s, row], local.at[s])

    q_local = pltpu.make_async_copy(q_in, qv, local.at[steps])
    p_local = pltpu.make_async_copy(p_in, pv, local.at[steps + 1])
    u_local = pltpu.make_async_copy(u_in, ug.at[col], local.at[steps + 2])
    v_local = pltpu.make_async_copy(v_in, vg.at[col], local.at[steps + 3])
    x_local(0).start()
    u_local.start()
    v_local.start()
    for s in range(1, steps):
        x_local(s).start()
    q_local.start()
    p_local.start()

    barrier = pltpu.get_barrier_semaphore()

    @pl.loop(0, n_row * n_col)
    def _(k):
        @pl.when(k != row * n_col + col)
        def _():
            pl.semaphore_signal(
                barrier, inc=1, device_id=(k // n_col, lax.rem(k, n_col)), device_id_type=MESH
            )

    pl.semaphore_wait(barrier, n_row * n_col - 1)

    def x_copy(s, k, way):
        target = {UP: row + 2, DOWN: row - 2, ACROSS: mate}[way]
        return pltpu.make_async_remote_copy(
            src_ref=xg.at[s, k], dst_ref=xg.at[s, k],
            send_sem=x_send.at[s, k, way], recv_sem=x_recv.at[s, k],
            device_id=(target, col), device_id_type=MESH,
        )

    def low_copy(s, k):
        return pltpu.make_async_remote_copy(
            src_ref=xg.at[s, k, :half], dst_ref=xg.at[s, k, :half],
            send_sem=x_send.at[s, k, ACROSS], recv_sem=x_recv.at[s, k],
            device_id=(mate, col), device_id_type=MESH,
        )

    def high_copy(s, k):
        return pltpu.make_async_remote_copy(
            src_ref=xg.at[s, k, half:], dst_ref=xg.at[s, k, half:],
            send_sem=h_send.at[s], recv_sem=h_recv.at[s],
            device_id=(twin, col), device_id_type=MESH,
        )

    def across(s, k, is_twin):
        @pl.when(is_twin)
        def _():
            low_copy(s, k).start()

        @pl.when(jnp.logical_not(is_twin))
        def _():
            x_copy(s, k, ACROSS).start()

    def own_sends(s):
        x_local(s).wait()
        x_copy(s, row, ACROSS).start()

        @pl.when(z + 1 < line)
        def _():
            x_copy(s, row, UP).start()

        @pl.when(z > 0)
        def _():
            x_copy(s, row, DOWN).start()

    def forward(s, d):
        @pl.when(z - d >= 0)
        def _():
            k = row - 2 * d
            x_copy(s, k, ACROSS).wait_recv()
            across(s, k, odd) if d == 1 else x_copy(s, k, ACROSS).start()

            @pl.when(z + 1 < line)
            def _():
                x_copy(s, k, UP).start()

        @pl.when(z + d < line)
        def _():
            k = row + 2 * d
            x_copy(s, k, ACROSS).wait_recv()
            across(s, k, jnp.logical_not(odd)) if d == 1 else x_copy(s, k, ACROSS).start()

            @pl.when(z > 0)
            def _():
                x_copy(s, k, DOWN).start()

    def uv_copy(which, d, slot):
        ref = (ug, vg)[which]
        return pltpu.make_async_remote_copy(
            src_ref=ref.at[slot], dst_ref=ref.at[slot],
            send_sem=uv_send.at[which, d], recv_sem=uv_recv.at[which, d],
            device_id=(row, lax.rem(col + d, n_col)), device_id_type=MESH,
        )

    own_sends(0)
    u_local.wait()
    v_local.wait()
    for d in range(1, n_col):
        uv_copy(0, d, col).start()
        uv_copy(1, d, col).start()
    for s in range(1, ahead):
        own_sends(s)

    q_local.wait()

    @pl.loop(0, t_rows * t_cols)
    def _(k):
        i, j = k // t_cols, lax.rem(k, t_cols)
        keep = lax.broadcasted_iota(jnp.int32, (rank_cap, u_rows), 0) < tile_rank[i, j]
        for b in range(order // u_rows):
            at = pl.ds(b * u_rows, u_rows)
            qt[i, j, :, at] = jnp.where(keep, qv[i, j, at, :].T, jnp.zeros((), BF16))

    p_local.wait()
    for d in range(1, n_col):
        slot = lax.rem(col + n_col - d, n_col)
        uv_copy(0, d, slot).wait_recv()
        uv_copy(1, d, slot).wait_recv()

    @pl.loop(0, t_rows)
    def _(i):
        keep = (
            lax.broadcasted_iota(jnp.int32, (rank_cap, u_rows), 0) < panel_rank[row * t_rows + i]
        )
        for b in range(n_col):
            at = pl.ds(b * u_rows, u_rows)
            ut[i, :, at] = jnp.where(keep, ug[b, i].T, jnp.zeros((), BF16))
            vt[i, :, at] = jnp.where(keep, vg[b, i].T, jnp.zeros((), BF16))

    def b_copy(s):
        return pltpu.make_async_remote_copy(
            src_ref=sbuf.at[s], dst_ref=rbuf.at[s],
            send_sem=b_send.at[s], recv_sem=b_recv.at[s],
            device_id=(row, owner(s)), device_id_type=MESH,
        )

    def sw_copy(s, k):
        return pltpu.make_async_remote_copy(
            src_ref=swb.at[s, k], dst_ref=swr.at[lax.rem(s, subs), row],
            send_sem=sw_send.at[s, k], recv_sem=sw_recv.at[lax.rem(s, subs), row],
            device_id=(k, owner(s)), device_id_type=MESH,
        )

    def compute(s):
        low_copy(s, twin + 1 - 2 * x).wait_recv()
        high_copy(s, twin + 1 - 2 * x).wait_recv()
        for e in range(1, line // 2):
            pair = lax.rem(z // 2 + e, line // 2)
            for b in range(2):
                x_copy(s, 2 * (2 * pair + b) + 1 - x, ACROSS).wait_recv()

        @pl.when(inside)
        def _():
            for i in range(t_rows):
                block = xg[s, :, first + i].reshape(order, width)
                proj = dot(ut[i], block).astype(BF16)
                term = dot(vg[:, i].reshape(order, rank_cap), proj)
                if i == 0:
                    sweep_acc[...] = term
                else:
                    sweep_acc[...] += term
            swb[s] = sweep_acc[...].astype(BF16).reshape(n_row, x_rows, width)

            @pl.loop(0, n_row)
            def _(k):
                mine = jnp.logical_and(k == row, s >= away)

                @pl.when(mine)
                def _():
                    swr[s - away, row] = swb[s, row]

                @pl.when(jnp.logical_not(mine))
                def _():
                    sw_copy(s, k).start()

        @pl.loop(0, t_rows)
        def _(i):
            total = None
            for j in range(t_cols):
                proj = dot(qt[i, j], xg[s, :, j].reshape(order, width)).astype(BF16)
                term = dot(pv[i, j], proj)
                total = term if total is None else total + term

            @pl.when(s < away)
            def _():
                sbuf[s, i] = total.astype(BF16)

            @pl.when(s >= away)
            def _():
                acc[lax.rem(s, subs), i] = total

        @pl.when(s < away)
        def _():
            b_copy(s).start()

    def reduce_sweep(h):
        for k in range(n_row):
            @pl.when(jnp.logical_not(jnp.logical_and(inside, k == row)))
            def _():
                pltpu.make_async_remote_copy(
                    src_ref=swr.at[h, k], dst_ref=swr.at[h, k],
                    send_sem=sw_send.at[h, k], recv_sem=sw_recv.at[h, k],
                    device_id=(row, col), device_id_type=MESH,
                ).wait_recv()

        total = swr[h, 0].astype(F32)
        for k in range(1, n_row):
            total = total + swr[h, k].astype(F32)
        swg[h, row] = total.astype(BF16)
        for d in range(1, n_row):
            g_copy(h, d, row).start()

    def g_copy(h, d, slot):
        return pltpu.make_async_remote_copy(
            src_ref=swg.at[h, slot], dst_ref=swg.at[h, slot],
            send_sem=g_send.at[h, d], recv_sem=g_recv.at[h, d],
            device_id=(lax.rem(row + d, n_row), col), device_id_type=MESH,
        )

    def add_received(h):
        for g in range(n_col - 1):
            b_copy(g * subs + h).wait_recv()

        @pl.loop(0, t_rows)
        def _(i):
            total = acc[h, i]
            for g in range(n_col - 1):
                total = total + rbuf[g * subs + h, i].astype(F32)
            acc[h, i] = total

    def finish(h):
        for d in range(1, n_row):
            g_copy(h, d, lax.rem(row + n_row - d, n_row)).wait_recv()

        @pl.loop(0, t_rows)
        def _(i):
            back = dot(vt[i], swg[h].reshape(order, width)).astype(BF16)
            late = dot(ug[:, i].reshape(order, rank_cap), back)
            out[i, :, h * width : (h + 1) * width] = (acc[h, i] - late).astype(BF16)

    @pl.loop(0, steps + 1)
    def _(s):
        @pl.when(s < steps)
        def _():
            forward(s, 1)
            x_copy(s, mate, ACROSS).wait_recv()
            high_copy(s, mate).start()

        @pl.when(s + ahead < steps)
        def _():
            own_sends(s + ahead)

        @pl.when(s == steps)
        def _():
            for h in range(subs - 1):
                reduce_sweep(h)

        @pl.when(s > 0)
        def _():
            compute(s - 1)

        @pl.when(s < steps)
        def _():
            for d in range(2, line):
                forward(s, d)

    reduce_sweep(subs - 1)
    for h in range(subs):
        add_received(h)
    for h in range(subs):
        finish(h)

    @pl.loop(0, steps)
    def _(s):
        for m in range(line):
            k = 2 * m + x
            @pl.when(k == twin)
            def _():
                low_copy(s, k).wait_send()

            @pl.when(k != twin)
            def _():
                x_copy(s, k, ACROSS).wait_send()

            @pl.when(jnp.logical_and(m <= z, z + 1 < line))
            def _():
                x_copy(s, k, UP).wait_send()

            @pl.when(jnp.logical_and(m >= z, z > 0))
            def _():
                x_copy(s, k, DOWN).wait_send()

        high_copy(s, mate).wait_send()

        @pl.when(s < away)
        def _():
            b_copy(s).wait_send()

        @pl.when(inside)
        def _():
            @pl.loop(0, n_row)
            def _(k):
                @pl.when(jnp.logical_not(jnp.logical_and(k == row, s >= away)))
                def _():
                    sw_copy(s, k).wait_send()

    for d in range(1, n_col):
        uv_copy(0, d, col).wait_send()
        uv_copy(1, d, col).wait_send()
    for h in range(subs):
        for d in range(1, n_row):
            g_copy(h, d, row).wait_send()


def shards(n_row, n_col, x_rhs, panel_u, panel_v, panel_rank, tile_p, tile_q, tile_rank):
    t_rows, t_cols, order, rank_cap = tile_p.shape
    x_rows, n_rhs = x_rhs.shape[1:]
    u_rows = panel_u.shape[1]
    width = n_rhs // n_col
    subs = 2
    part = width // subs
    steps = n_col * subs
    away = steps - subs
    fits = (
        n_rhs % n_col == 0
        and width % (128 * subs) == 0
        and x_rows % 16 == 0
        and u_rows % 128 == 0
        and n_row % 4 == 0
        and n_col > 1
        and t_cols % t_rows == 0
        and t_cols % 2 == 0
    )
    if not fits:
        return plain(x_rhs, panel_u, panel_v, panel_rank, tile_p, tile_q, tile_rank)
    dma = pltpu.SemaphoreType.DMA
    flops = 4 * order * rank_cap * n_rhs * t_rows * (t_cols + 1)
    return pl.pallas_call(
        functools.partial(kernel, n_row, n_col),
        out_shape=jax.ShapeDtypeStruct((t_rows, order, width), BF16),
        in_specs=[pl.BlockSpec(memory_space=pltpu.SMEM)] * 2
        + [pl.BlockSpec(memory_space=pl.ANY)] * 5,
        out_specs=pl.BlockSpec(memory_space=pltpu.VMEM),
        scratch_shapes=[
            pltpu.VMEM((steps, n_row, t_cols, x_rows, part), BF16),
            pltpu.VMEM(tile_p.shape, BF16),
            pltpu.VMEM(tile_q.shape, BF16),
            pltpu.VMEM((t_rows, t_cols, rank_cap, order), BF16),
            pltpu.VMEM((n_col, t_rows, u_rows, rank_cap), BF16),
            pltpu.VMEM((n_col, t_rows, u_rows, rank_cap), BF16),
            pltpu.VMEM((t_rows, rank_cap, order), BF16),
            pltpu.VMEM((t_rows, rank_cap, order), BF16),
            pltpu.VMEM((subs, t_rows, order, part), F32),
            pltpu.VMEM((order, part), F32),
            pltpu.VMEM((away, t_rows, order, part), BF16),
            pltpu.VMEM((away, t_rows, order, part), BF16),
            pltpu.VMEM((steps, n_row, x_rows, part), BF16),
            pltpu.VMEM((subs, n_row, x_rows, part), BF16),
            pltpu.VMEM((subs, n_row, x_rows, part), BF16),
            dma((steps, n_row, 3)),
            dma((steps, n_row)),
            dma((steps,)),
            dma((steps,)),
            dma((2, n_col)),
            dma((2, n_col)),
            dma((away,)),
            dma((away,)),
            dma((steps, n_row)),
            dma((subs, n_row)),
            dma((subs, n_row)),
            dma((subs, n_row)),
            dma((steps + 4,)),
        ],
        compiler_params=pltpu.CompilerParams(
            collective_id=0, has_side_effects=True, vmem_limit_bytes=56 * 2**20
        ),
        cost_estimate=pl.CostEstimate(flops=flops, bytes_accessed=20 * 2**20, transcendentals=0),
    )(tile_rank, panel_rank, x_rhs, panel_u, panel_v, tile_p, tile_q)


def solution(mesh):
    return jax.shard_map(
        functools.partial(shards, mesh.shape["row"], mesh.shape["col"]),
        mesh=mesh,
        in_specs=(
            P("col", "row", None),
            P("row", "col", None),
            P("row", "col", None),
            P(),
            P("row", "col", None, None),
            P("row", "col", None, None),
            P("row", "col"),
        ),
        out_specs=P("row", None, "col"),
        check_vma=False,
    )
```

```python
import functools

import jax
import jax.numpy as jnp
from jax import lax
from jax.experimental import pallas as pl
from jax.experimental.pallas import tpu as pltpu
from jax.sharding import PartitionSpec as P

BF16 = jnp.bfloat16
F32 = jnp.float32
MESH = pl.DeviceIdType.MESH
UP, DOWN, ACROSS = 0, 1, 2


def plain(x_rhs, panel_u, panel_v, panel_rank, tile_p, tile_q, tile_rank):
    exact = lax.Precision.HIGHEST
    row_at = lax.axis_index("row")
    col_at = lax.axis_index("col")
    t_rows = tile_p.shape[0]
    t_cols = tile_p.shape[1]
    rank_cap = tile_p.shape[3]
    gathered = lax.all_gather(x_rhs, "row", axis=1, tiled=True)
    full_u, full_v = (
        lax.all_gather(panel_u, "col", axis=1, tiled=True),
        lax.all_gather(panel_v, "col", axis=1, tiled=True),
    )
    tile_slot = lax.broadcasted_iota(jnp.int32, (1, 1, rank_cap, 1), 2)
    tile_proj = jnp.einsum("ijbr,jbn->ijrn", tile_q, gathered, preferred_element_type=jnp.float32)
    tile_proj = jnp.where(tile_slot < tile_rank[:, :, None, None], tile_proj, 0.0).astype(
        jnp.bfloat16
    )
    base_sum = jnp.einsum("ijbr,ijrn->ibn", tile_p, tile_proj, preferred_element_type=jnp.float32)
    rank_slot = lax.broadcasted_iota(jnp.int32, (1, rank_cap, 1), 1)
    row_rank = lax.dynamic_slice_in_dim(panel_rank, row_at * t_rows, t_rows)
    row_keep = rank_slot < row_rank[:, None, None]
    u_wide = full_u.astype(jnp.float32)
    tile_ids = row_at * t_rows + jnp.arange(t_rows, dtype=jnp.int32)
    inside = tile_ids // t_cols == col_at
    where_rhs = jnp.clip(tile_ids - col_at * t_cols, 0, t_cols - 1)
    picked = jnp.take(gathered, where_rhs, axis=0)
    keep = jnp.logical_and(inside[:, None, None], row_keep)
    panel_proj = jnp.einsum("jbr,jbn->jrn", full_u, picked, preferred_element_type=jnp.float32)
    panel_proj = jnp.where(keep, panel_proj, 0.0).astype(jnp.bfloat16)
    sweep_part = jnp.einsum("jbr,jrn->bn", full_v, panel_proj, preferred_element_type=jnp.float32)
    sweep_share = lax.psum_scatter(
        sweep_part.astype(jnp.bfloat16), "col", scatter_dimension=1, tiled=True
    )
    sweep = lax.psum(sweep_share, "row").astype(jnp.float32)
    back_proj = jnp.einsum("ibr,bn->irn", full_v.astype(jnp.float32), sweep, precision=exact)
    back_proj = jnp.where(row_keep, back_proj, 0.0)
    late_term = jnp.einsum("ibr,irn->ibn", u_wide, back_proj, precision=exact)
    summed = lax.psum_scatter(
        base_sum.astype(jnp.bfloat16), "col", scatter_dimension=2, tiled=True
    ).astype(jnp.float32)
    return (summed - late_term).astype(jnp.bfloat16)


def dot(a, b):
    return jnp.dot(a, b, preferred_element_type=F32)


def kernel(
    n_row, n_col,
    tile_rank, panel_rank, x_in, u_in, v_in, p_in, q_in,
    out,
    xg, pv, qv, qt, ug, vg, ut, vt, acc, sweep_acc, sbuf, rbuf, swb, swr, swg,
    x_send, x_recv, h_send, h_recv, uv_send, uv_recv, b_send, b_recv, sw_send, sw_recv, g_send, g_recv, local,
):
    t_rows, t_cols, order, rank_cap = pv.shape
    x_rows = xg.shape[3]
    width = xg.shape[4]
    u_rows = ug.shape[2]
    subs = swr.shape[0]
    steps = n_col * subs
    away = steps - subs
    ahead = 2
    half = t_cols // 2
    line = n_row // 2
    row = lax.axis_index("row")
    col = lax.axis_index("col")
    z, x = row // 2, row % 2
    mate = row + 1 - 2 * x
    odd = z % 2 == 1
    twin = row + 2 - 4 * (z % 2)
    inside = (row * t_rows) // t_cols == col
    first = lax.rem(row * t_rows, t_cols)

    def owner(s):
        return lax.rem(col + 1 + s // subs, n_col)

    def x_local(s):
        at = pl.multiple_of((owner(s) * subs + lax.rem(s, subs)) * width, width)
        return pltpu.make_async_copy(x_in.at[:, :, pl.ds(at, width)], xg.at[s, row], local.at[s])

    q_local = pltpu.make_async_copy(q_in, qv, local.at[steps])
    p_local = pltpu.make_async_copy(p_in, pv, local.at[steps + 1])
    u_local = pltpu.make_async_copy(u_in, ug.at[col], local.at[steps + 2])
    v_local = pltpu.make_async_copy(v_in, vg.at[col], local.at[steps + 3])
    x_local(0).start()
    u_local.start()
    v_local.start()
    for s in range(1, steps):
        x_local(s).start()
    q_local.start()
    p_local.start()

    barrier = pltpu.get_barrier_semaphore()

    @pl.loop(0, n_row * n_col)
    def _(k):
        @pl.when(k != row * n_col + col)
        def _():
            pl.semaphore_signal(
                barrier, inc=1, device_id=(k // n_col, lax.rem(k, n_col)), device_id_type=MESH
            )

    pl.semaphore_wait(barrier, n_row * n_col - 1)

    def x_copy(s, k, way):
        target = {UP: row + 2, DOWN: row - 2, ACROSS: mate}[way]
        return pltpu.make_async_remote_copy(
            src_ref=xg.at[s, k], dst_ref=xg.at[s, k],
            send_sem=x_send.at[s, k, way], recv_sem=x_recv.at[s, k],
            device_id=(target, col), device_id_type=MESH,
        )

    def low_copy(s, k):
        return pltpu.make_async_remote_copy(
            src_ref=xg.at[s, k, :half], dst_ref=xg.at[s, k, :half],
            send_sem=x_send.at[s, k, ACROSS], recv_sem=x_recv.at[s, k],
            device_id=(mate, col), device_id_type=MESH,
        )

    def high_copy(s, k):
        return pltpu.make_async_remote_copy(
            src_ref=xg.at[s, k, half:], dst_ref=xg.at[s, k, half:],
            send_sem=h_send.at[s], recv_sem=h_recv.at[s],
            device_id=(twin, col), device_id_type=MESH,
        )

    def across(s, k, is_twin):
        @pl.when(is_twin)
        def _():
            low_copy(s, k).start()

        @pl.when(jnp.logical_not(is_twin))
        def _():
            x_copy(s, k, ACROSS).start()

    def own_sends(s):
        x_local(s).wait()
        x_copy(s, row, ACROSS).start()

        @pl.when(z + 1 < line)
        def _():
            x_copy(s, row, UP).start()

        @pl.when(z > 0)
        def _():
            x_copy(s, row, DOWN).start()

    def forward(s, d):
        @pl.when(z - d >= 0)
        def _():
            k = row - 2 * d
            x_copy(s, k, ACROSS).wait_recv()
            across(s, k, odd) if d == 1 else x_copy(s, k, ACROSS).start()

            @pl.when(z + 1 < line)
            def _():
                x_copy(s, k, UP).start()

        @pl.when(z + d < line)
        def _():
            k = row + 2 * d
            x_copy(s, k, ACROSS).wait_recv()
            across(s, k, jnp.logical_not(odd)) if d == 1 else x_copy(s, k, ACROSS).start()

            @pl.when(z > 0)
            def _():
                x_copy(s, k, DOWN).start()

    def uv_copy(which, d, slot):
        ref = (ug, vg)[which]
        return pltpu.make_async_remote_copy(
            src_ref=ref.at[slot], dst_ref=ref.at[slot],
            send_sem=uv_send.at[which, d], recv_sem=uv_recv.at[which, d],
            device_id=(row, lax.rem(col + d, n_col)), device_id_type=MESH,
        )

    own_sends(0)
    u_local.wait()
    v_local.wait()
    for d in range(1, n_col):
        uv_copy(0, d, col).start()
        uv_copy(1, d, col).start()
    for s in range(1, ahead):
        own_sends(s)

    q_local.wait()

    @pl.loop(0, t_rows * t_cols)
    def _(k):
        i, j = k // t_cols, lax.rem(k, t_cols)
        keep = lax.broadcasted_iota(jnp.int32, (rank_cap, u_rows), 0) < tile_rank[i, j]
        for b in range(order // u_rows):
            at = pl.ds(b * u_rows, u_rows)
            qt[i, j, :, at] = jnp.where(keep, qv[i, j, at, :].T, jnp.zeros((), BF16))

    p_local.wait()
    for d in range(1, n_col):
        slot = lax.rem(col + n_col - d, n_col)
        uv_copy(0, d, slot).wait_recv()
        uv_copy(1, d, slot).wait_recv()

    @pl.loop(0, t_rows)
    def _(i):
        keep = (
            lax.broadcasted_iota(jnp.int32, (rank_cap, u_rows), 0) < panel_rank[row * t_rows + i]
        )
        for b in range(n_col):
            at = pl.ds(b * u_rows, u_rows)
            ut[i, :, at] = jnp.where(keep, ug[b, i].T, jnp.zeros((), BF16))
            vt[i, :, at] = jnp.where(keep, vg[b, i].T, jnp.zeros((), BF16))

    def b_copy(s):
        return pltpu.make_async_remote_copy(
            src_ref=sbuf.at[s], dst_ref=rbuf.at[s],
            send_sem=b_send.at[s], recv_sem=b_recv.at[s],
            device_id=(row, owner(s)), device_id_type=MESH,
        )

    def sw_copy(s, k):
        return pltpu.make_async_remote_copy(
            src_ref=swb.at[s, k], dst_ref=swr.at[lax.rem(s, subs), row],
            send_sem=sw_send.at[s, k], recv_sem=sw_recv.at[lax.rem(s, subs), row],
            device_id=(k, owner(s)), device_id_type=MESH,
        )

    def compute(s):
        low_copy(s, twin + 1 - 2 * x).wait_recv()
        high_copy(s, twin + 1 - 2 * x).wait_recv()
        for e in range(1, line // 2):
            pair = lax.rem(z // 2 + e, line // 2)
            for b in range(2):
                x_copy(s, 2 * (2 * pair + b) + 1 - x, ACROSS).wait_recv()

        @pl.when(inside)
        def _():
            for i in range(t_rows):
                block = xg[s, :, first + i].reshape(order, width)
                proj = dot(ut[i], block).astype(BF16)
                term = dot(vg[:, i].reshape(order, rank_cap), proj)
                if i == 0:
                    sweep_acc[...] = term
                else:
                    sweep_acc[...] += term
            swb[s] = sweep_acc[...].astype(BF16).reshape(n_row, x_rows, width)

            @pl.loop(0, n_row)
            def _(k):
                mine = jnp.logical_and(k == row, s >= away)

                @pl.when(mine)
                def _():
                    swr[s - away, row] = swb[s, row]

                @pl.when(jnp.logical_not(mine))
                def _():
                    sw_copy(s, k).start()

        @pl.loop(0, t_rows)
        def _(i):
            total = None
            for j in range(t_cols):
                proj = dot(qt[i, j], xg[s, :, j].reshape(order, width)).astype(BF16)
                term = dot(pv[i, j], proj)
                total = term if total is None else total + term

            @pl.when(s < away)
            def _():
                sbuf[s, i] = total.astype(BF16)

            @pl.when(s >= away)
            def _():
                acc[lax.rem(s, subs), i] = total

        @pl.when(s < away)
        def _():
            b_copy(s).start()

    def reduce_sweep(h):
        for k in range(n_row):
            @pl.when(jnp.logical_not(jnp.logical_and(inside, k == row)))
            def _():
                pltpu.make_async_remote_copy(
                    src_ref=swr.at[h, k], dst_ref=swr.at[h, k],
                    send_sem=sw_send.at[h, k], recv_sem=sw_recv.at[h, k],
                    device_id=(row, col), device_id_type=MESH,
                ).wait_recv()

        total = swr[h, 0].astype(F32)
        for k in range(1, n_row):
            total = total + swr[h, k].astype(F32)
        swg[h, row] = total.astype(BF16)
        for d in range(1, n_row):
            g_copy(h, d, row).start()

    def g_copy(h, d, slot):
        return pltpu.make_async_remote_copy(
            src_ref=swg.at[h, slot], dst_ref=swg.at[h, slot],
            send_sem=g_send.at[h, d], recv_sem=g_recv.at[h, d],
            device_id=(lax.rem(row + d, n_row), col), device_id_type=MESH,
        )

    def add_received(h):
        for g in range(n_col - 1):
            b_copy(g * subs + h).wait_recv()

        @pl.loop(0, t_rows)
        def _(i):
            total = acc[h, i]
            for g in range(n_col - 1):
                total = total + rbuf[g * subs + h, i].astype(F32)
            acc[h, i] = total

    def finish(h):
        for d in range(1, n_row):
            g_copy(h, d, lax.rem(row + n_row - d, n_row)).wait_recv()

        @pl.loop(0, t_rows)
        def _(i):
            back = dot(vt[i], swg[h].reshape(order, width)).astype(BF16)
            late = dot(ug[:, i].reshape(order, rank_cap), back)
            out[i, :, h * width : (h + 1) * width] = (acc[h, i] - late).astype(BF16)

    @pl.loop(0, steps + 1)
    def _(s):
        @pl.when(s < steps)
        def _():
            forward(s, 1)
            x_copy(s, mate, ACROSS).wait_recv()
            high_copy(s, mate).start()

        @pl.when(s + ahead < steps)
        def _():
            own_sends(s + ahead)

        @pl.when(s == steps)
        def _():
            for h in range(subs - 1):
                reduce_sweep(h)

        @pl.when(s > 0)
        def _():
            compute(s - 1)

        @pl.when(s < steps)
        def _():
            for d in range(2, line):
                forward(s, d)

    reduce_sweep(subs - 1)
    for h in range(subs):
        add_received(h)
    for h in range(subs):
        finish(h)

    @pl.loop(0, steps)
    def _(s):
        for m in range(line):
            k = 2 * m + x
            @pl.when(k == twin)
            def _():
                low_copy(s, k).wait_send()

            @pl.when(k != twin)
            def _():
                x_copy(s, k, ACROSS).wait_send()

            @pl.when(jnp.logical_and(m <= z, z + 1 < line))
            def _():
                x_copy(s, k, UP).wait_send()

            @pl.when(jnp.logical_and(m >= z, z > 0))
            def _():
                x_copy(s, k, DOWN).wait_send()

        high_copy(s, mate).wait_send()

        @pl.when(s < away)
        def _():
            b_copy(s).wait_send()

        @pl.when(inside)
        def _():
            @pl.loop(0, n_row)
            def _(k):
                @pl.when(jnp.logical_not(jnp.logical_and(k == row, s >= away)))
                def _():
                    sw_copy(s, k).wait_send()

    for d in range(1, n_col):
        uv_copy(0, d, col).wait_send()
        uv_copy(1, d, col).wait_send()
    for h in range(subs):
        for d in range(1, n_row):
            g_copy(h, d, row).wait_send()


def shards(n_row, n_col, x_rhs, panel_u, panel_v, panel_rank, tile_p, tile_q, tile_rank):
    t_rows, t_cols, order, rank_cap = tile_p.shape
    x_rows, n_rhs = x_rhs.shape[1:]
    u_rows = panel_u.shape[1]
    width = n_rhs // n_col
    subs = 1
    part = width // subs
    steps = n_col * subs
    away = steps - subs
    fits = (
        n_rhs % n_col == 0
        and width % (128 * subs) == 0
        and x_rows % 16 == 0
        and u_rows % 128 == 0
        and n_row % 4 == 0
        and n_col > 1
        and t_cols % t_rows == 0
        and t_cols % 2 == 0
    )
    if not fits:
        return plain(x_rhs, panel_u, panel_v, panel_rank, tile_p, tile_q, tile_rank)
    dma = pltpu.SemaphoreType.DMA
    flops = 4 * order * rank_cap * n_rhs * t_rows * (t_cols + 1)
    return pl.pallas_call(
        functools.partial(kernel, n_row, n_col),
        out_shape=jax.ShapeDtypeStruct((t_rows, order, width), BF16),
        in_specs=[pl.BlockSpec(memory_space=pltpu.SMEM)] * 2
        + [pl.BlockSpec(memory_space=pl.ANY)] * 5,
        out_specs=pl.BlockSpec(memory_space=pltpu.VMEM),
        scratch_shapes=[
            pltpu.VMEM((steps, n_row, t_cols, x_rows, part), BF16),
            pltpu.VMEM(tile_p.shape, BF16),
            pltpu.VMEM(tile_q.shape, BF16),
            pltpu.VMEM((t_rows, t_cols, rank_cap, order), BF16),
            pltpu.VMEM((n_col, t_rows, u_rows, rank_cap), BF16),
            pltpu.VMEM((n_col, t_rows, u_rows, rank_cap), BF16),
            pltpu.VMEM((t_rows, rank_cap, order), BF16),
            pltpu.VMEM((t_rows, rank_cap, order), BF16),
            pltpu.VMEM((subs, t_rows, order, part), F32),
            pltpu.VMEM((order, part), F32),
            pltpu.VMEM((away, t_rows, order, part), BF16),
            pltpu.VMEM((away, t_rows, order, part), BF16),
            pltpu.VMEM((steps, n_row, x_rows, part), BF16),
            pltpu.VMEM((subs, n_row, x_rows, part), BF16),
            pltpu.VMEM((subs, n_row, x_rows, part), BF16),
            dma((steps, n_row, 3)),
            dma((steps, n_row)),
            dma((steps,)),
            dma((steps,)),
            dma((2, n_col)),
            dma((2, n_col)),
            dma((away,)),
            dma((away,)),
            dma((steps, n_row)),
            dma((subs, n_row)),
            dma((subs, n_row)),
            dma((subs, n_row)),
            dma((steps + 4,)),
        ],
        compiler_params=pltpu.CompilerParams(
            collective_id=0, has_side_effects=True, vmem_limit_bytes=56 * 2**20
        ),
        cost_estimate=pl.CostEstimate(flops=flops, bytes_accessed=20 * 2**20, transcendentals=0),
    )(tile_rank, panel_rank, x_rhs, panel_u, panel_v, tile_p, tile_q)


def solution(mesh):
    return jax.shard_map(
        functools.partial(shards, mesh.shape["row"], mesh.shape["col"]),
        mesh=mesh,
        in_specs=(
            P("col", "row", None),
            P("row", "col", None),
            P("row", "col", None),
            P(),
            P("row", "col", None, None),
            P("row", "col", None, None),
            P("row", "col"),
        ),
        out_specs=P("row", None, "col"),
        check_vma=False,
    )
```

```python
import functools

import jax
import jax.numpy as jnp
from jax import lax
from jax.experimental import pallas as pl
from jax.experimental.pallas import tpu as pltpu
from jax.sharding import PartitionSpec as P

BF16 = jnp.bfloat16
F32 = jnp.float32
MESH = pl.DeviceIdType.MESH
UP, DOWN, ACROSS = 0, 1, 2


def plain(x_rhs, panel_u, panel_v, panel_rank, tile_p, tile_q, tile_rank):
    exact = lax.Precision.HIGHEST
    row_at = lax.axis_index("row")
    col_at = lax.axis_index("col")
    t_rows = tile_p.shape[0]
    t_cols = tile_p.shape[1]
    rank_cap = tile_p.shape[3]
    gathered = lax.all_gather(x_rhs, "row", axis=1, tiled=True)
    full_u, full_v = (
        lax.all_gather(panel_u, "col", axis=1, tiled=True),
        lax.all_gather(panel_v, "col", axis=1, tiled=True),
    )
    tile_slot = lax.broadcasted_iota(jnp.int32, (1, 1, rank_cap, 1), 2)
    tile_proj = jnp.einsum("ijbr,jbn->ijrn", tile_q, gathered, preferred_element_type=jnp.float32)
    tile_proj = jnp.where(tile_slot < tile_rank[:, :, None, None], tile_proj, 0.0).astype(
        jnp.bfloat16
    )
    base_sum = jnp.einsum("ijbr,ijrn->ibn", tile_p, tile_proj, preferred_element_type=jnp.float32)
    rank_slot = lax.broadcasted_iota(jnp.int32, (1, rank_cap, 1), 1)
    row_rank = lax.dynamic_slice_in_dim(panel_rank, row_at * t_rows, t_rows)
    row_keep = rank_slot < row_rank[:, None, None]
    u_wide = full_u.astype(jnp.float32)
    tile_ids = row_at * t_rows + jnp.arange(t_rows, dtype=jnp.int32)
    inside = tile_ids // t_cols == col_at
    where_rhs = jnp.clip(tile_ids - col_at * t_cols, 0, t_cols - 1)
    picked = jnp.take(gathered, where_rhs, axis=0)
    keep = jnp.logical_and(inside[:, None, None], row_keep)
    panel_proj = jnp.einsum("jbr,jbn->jrn", full_u, picked, preferred_element_type=jnp.float32)
    panel_proj = jnp.where(keep, panel_proj, 0.0).astype(jnp.bfloat16)
    sweep_part = jnp.einsum("jbr,jrn->bn", full_v, panel_proj, preferred_element_type=jnp.float32)
    sweep_share = lax.psum_scatter(
        sweep_part.astype(jnp.bfloat16), "col", scatter_dimension=1, tiled=True
    )
    sweep = lax.psum(sweep_share, "row").astype(jnp.float32)
    back_proj = jnp.einsum("ibr,bn->irn", full_v.astype(jnp.float32), sweep, precision=exact)
    back_proj = jnp.where(row_keep, back_proj, 0.0)
    late_term = jnp.einsum("ibr,irn->ibn", u_wide, back_proj, precision=exact)
    summed = lax.psum_scatter(
        base_sum.astype(jnp.bfloat16), "col", scatter_dimension=2, tiled=True
    ).astype(jnp.float32)
    return (summed - late_term).astype(jnp.bfloat16)


def dot(a, b):
    return jnp.dot(a, b, preferred_element_type=F32)


def kernel(
    n_row, n_col,
    tile_rank, panel_rank, x_in, u_in, v_in, p_in, q_in,
    out,
    xg, pv, qv, qt, ug, vg, ut, vt, acc, sweep_acc, sbuf, rbuf, swb, swr, swg,
    x_send, x_recv, h_send, h_recv, uv_send, uv_recv, b_send, b_recv, sw_send, sw_recv, g_send, g_recv, local,
):
    t_rows, t_cols, order, rank_cap = pv.shape
    x_rows = xg.shape[3]
    width = xg.shape[4]
    u_rows = ug.shape[2]
    subs = swr.shape[0]
    steps = n_col * subs
    away = steps - subs
    ahead = 2
    half = t_cols // 2
    line = n_row // 2
    row = lax.axis_index("row")
    col = lax.axis_index("col")
    z, x = row // 2, row % 2
    mate = row + 1 - 2 * x
    odd = z % 2 == 1
    twin = row + 2 - 4 * (z % 2)
    inside = (row * t_rows) // t_cols == col
    first = lax.rem(row * t_rows, t_cols)

    def owner(s):
        flip = n_col - 1 - s // subs
        bits = [1 << b for b in range(n_col.bit_length() - 1)]
        return sum(lax.rem(col // b + flip // b, 2) * b for b in bits)

    def x_local(s):
        at = pl.multiple_of((owner(s) * subs + lax.rem(s, subs)) * width, width)
        return pltpu.make_async_copy(x_in.at[:, :, pl.ds(at, width)], xg.at[s, row], local.at[s])

    q_local = pltpu.make_async_copy(q_in, qv, local.at[steps])
    p_local = pltpu.make_async_copy(p_in, pv, local.at[steps + 1])
    u_local = pltpu.make_async_copy(u_in, ug.at[col], local.at[steps + 2])
    v_local = pltpu.make_async_copy(v_in, vg.at[col], local.at[steps + 3])
    x_local(0).start()
    u_local.start()
    v_local.start()
    for s in range(1, steps):
        x_local(s).start()
    q_local.start()
    p_local.start()

    barrier = pltpu.get_barrier_semaphore()

    @pl.loop(0, n_row * n_col)
    def _(k):
        @pl.when(k != row * n_col + col)
        def _():
            pl.semaphore_signal(
                barrier, inc=1, device_id=(k // n_col, lax.rem(k, n_col)), device_id_type=MESH
            )

    pl.semaphore_wait(barrier, n_row * n_col - 1)

    def x_copy(s, k, way):
        target = {UP: row + 2, DOWN: row - 2, ACROSS: mate}[way]
        return pltpu.make_async_remote_copy(
            src_ref=xg.at[s, k], dst_ref=xg.at[s, k],
            send_sem=x_send.at[s, k, way], recv_sem=x_recv.at[s, k],
            device_id=(target, col), device_id_type=MESH,
        )

    def low_copy(s, k):
        return pltpu.make_async_remote_copy(
            src_ref=xg.at[s, k, :half], dst_ref=xg.at[s, k, :half],
            send_sem=x_send.at[s, k, ACROSS], recv_sem=x_recv.at[s, k],
            device_id=(mate, col), device_id_type=MESH,
        )

    def high_copy(s, k):
        return pltpu.make_async_remote_copy(
            src_ref=xg.at[s, k, half:], dst_ref=xg.at[s, k, half:],
            send_sem=h_send.at[s], recv_sem=h_recv.at[s],
            device_id=(twin, col), device_id_type=MESH,
        )

    def across(s, k, is_twin):
        @pl.when(is_twin)
        def _():
            low_copy(s, k).start()

        @pl.when(jnp.logical_not(is_twin))
        def _():
            x_copy(s, k, ACROSS).start()

    def own_sends(s):
        x_local(s).wait()
        x_copy(s, row, ACROSS).start()

        @pl.when(z + 1 < line)
        def _():
            x_copy(s, row, UP).start()

        @pl.when(z > 0)
        def _():
            x_copy(s, row, DOWN).start()

    def forward(s, d):
        @pl.when(z - d >= 0)
        def _():
            k = row - 2 * d
            x_copy(s, k, ACROSS).wait_recv()
            across(s, k, odd) if d == 1 else x_copy(s, k, ACROSS).start()

            @pl.when(z + 1 < line)
            def _():
                x_copy(s, k, UP).start()

        @pl.when(z + d < line)
        def _():
            k = row + 2 * d
            x_copy(s, k, ACROSS).wait_recv()
            across(s, k, jnp.logical_not(odd)) if d == 1 else x_copy(s, k, ACROSS).start()

            @pl.when(z > 0)
            def _():
                x_copy(s, k, DOWN).start()

    def uv_copy(which, d, slot):
        ref = (ug, vg)[which]
        return pltpu.make_async_remote_copy(
            src_ref=ref.at[slot], dst_ref=ref.at[slot],
            send_sem=uv_send.at[which, d], recv_sem=uv_recv.at[which, d],
            device_id=(row, lax.rem(col + d, n_col)), device_id_type=MESH,
        )

    own_sends(0)
    u_local.wait()
    v_local.wait()
    for d in range(1, n_col):
        uv_copy(0, d, col).start()
        uv_copy(1, d, col).start()
    for s in range(1, ahead):
        own_sends(s)

    q_local.wait()

    @pl.loop(0, t_rows * t_cols)
    def _(k):
        i, j = k // t_cols, lax.rem(k, t_cols)
        keep = lax.broadcasted_iota(jnp.int32, (rank_cap, u_rows), 0) < tile_rank[i, j]
        for b in range(order // u_rows):
            at = pl.ds(b * u_rows, u_rows)
            qt[i, j, :, at] = jnp.where(keep, qv[i, j, at, :].T, jnp.zeros((), BF16))

    p_local.wait()
    for d in range(1, n_col):
        slot = lax.rem(col + n_col - d, n_col)
        uv_copy(0, d, slot).wait_recv()
        uv_copy(1, d, slot).wait_recv()

    @pl.loop(0, t_rows)
    def _(i):
        keep = (
            lax.broadcasted_iota(jnp.int32, (rank_cap, u_rows), 0) < panel_rank[row * t_rows + i]
        )
        for b in range(n_col):
            at = pl.ds(b * u_rows, u_rows)
            ut[i, :, at] = jnp.where(keep, ug[b, i].T, jnp.zeros((), BF16))
            vt[i, :, at] = jnp.where(keep, vg[b, i].T, jnp.zeros((), BF16))

    def b_copy(s):
        return pltpu.make_async_remote_copy(
            src_ref=sbuf.at[s], dst_ref=rbuf.at[s],
            send_sem=b_send.at[s], recv_sem=b_recv.at[s],
            device_id=(row, owner(s)), device_id_type=MESH,
        )

    def sw_copy(s, k):
        return pltpu.make_async_remote_copy(
            src_ref=swb.at[s, k], dst_ref=swr.at[lax.rem(s, subs), row],
            send_sem=sw_send.at[s, k], recv_sem=sw_recv.at[lax.rem(s, subs), row],
            device_id=(k, owner(s)), device_id_type=MESH,
        )

    def compute(s):
        low_copy(s, twin + 1 - 2 * x).wait_recv()
        high_copy(s, twin + 1 - 2 * x).wait_recv()
        for e in range(1, line // 2):
            pair = lax.rem(z // 2 + e, line // 2)
            for b in range(2):
                x_copy(s, 2 * (2 * pair + b) + 1 - x, ACROSS).wait_recv()

        @pl.when(inside)
        def _():
            for i in range(t_rows):
                block = xg[s, :, first + i].reshape(order, width)
                proj = dot(ut[i], block).astype(BF16)
                term = dot(vg[:, i].reshape(order, rank_cap), proj)
                if i == 0:
                    sweep_acc[...] = term
                else:
                    sweep_acc[...] += term
            swb[s] = sweep_acc[...].astype(BF16).reshape(n_row, x_rows, width)

            @pl.loop(0, n_row)
            def _(k):
                mine = jnp.logical_and(k == row, s >= away)

                @pl.when(mine)
                def _():
                    swr[s - away, row] = swb[s, row]

                @pl.when(jnp.logical_not(mine))
                def _():
                    sw_copy(s, k).start()

        @pl.loop(0, t_rows)
        def _(i):
            total = None
            for j in range(t_cols):
                proj = dot(qt[i, j], xg[s, :, j].reshape(order, width)).astype(BF16)
                term = dot(pv[i, j], proj)
                total = term if total is None else total + term

            @pl.when(s < away)
            def _():
                sbuf[s, i] = total.astype(BF16)

            @pl.when(s >= away)
            def _():
                acc[lax.rem(s, subs), i] = total

        @pl.when(s < away)
        def _():
            b_copy(s).start()

    def reduce_sweep(h):
        for k in range(n_row):
            @pl.when(jnp.logical_not(jnp.logical_and(inside, k == row)))
            def _():
                pltpu.make_async_remote_copy(
                    src_ref=swr.at[h, k], dst_ref=swr.at[h, k],
                    send_sem=sw_send.at[h, k], recv_sem=sw_recv.at[h, k],
                    device_id=(row, col), device_id_type=MESH,
                ).wait_recv()

        total = swr[h, 0].astype(F32)
        for k in range(1, n_row):
            total = total + swr[h, k].astype(F32)
        swg[h, row] = total.astype(BF16)
        for d in range(1, n_row):
            g_copy(h, d, row).start()

    def g_copy(h, d, slot):
        return pltpu.make_async_remote_copy(
            src_ref=swg.at[h, slot], dst_ref=swg.at[h, slot],
            send_sem=g_send.at[h, d], recv_sem=g_recv.at[h, d],
            device_id=(lax.rem(row + d, n_row), col), device_id_type=MESH,
        )

    def add_received(h):
        for g in range(n_col - 1):
            b_copy(g * subs + h).wait_recv()

        @pl.loop(0, t_rows)
        def _(i):
            total = acc[h, i]
            for g in range(n_col - 1):
                total = total + rbuf[g * subs + h, i].astype(F32)
            acc[h, i] = total

    def finish(h):
        for d in range(1, n_row):
            g_copy(h, d, lax.rem(row + n_row - d, n_row)).wait_recv()

        @pl.loop(0, t_rows)
        def _(i):
            back = dot(vt[i], swg[h].reshape(order, width)).astype(BF16)
            late = dot(ug[:, i].reshape(order, rank_cap), back)
            out[i, :, h * width : (h + 1) * width] = (acc[h, i] - late).astype(BF16)

    @pl.loop(0, steps + 1)
    def _(s):
        @pl.when(s < steps)
        def _():
            forward(s, 1)
            x_copy(s, mate, ACROSS).wait_recv()
            high_copy(s, mate).start()

        @pl.when(s + ahead < steps)
        def _():
            own_sends(s + ahead)

        @pl.when(s == steps)
        def _():
            for h in range(subs - 1):
                reduce_sweep(h)

        @pl.when(s < steps)
        def _():
            for d in range(2, line):
                forward(s, d)

        @pl.when(s > 0)
        def _():
            compute(s - 1)

    reduce_sweep(subs - 1)
    for h in range(subs):
        add_received(h)
    for h in range(subs):
        finish(h)

    @pl.loop(0, steps)
    def _(s):
        for m in range(line):
            k = 2 * m + x
            @pl.when(k == twin)
            def _():
                low_copy(s, k).wait_send()

            @pl.when(k != twin)
            def _():
                x_copy(s, k, ACROSS).wait_send()

            @pl.when(jnp.logical_and(m <= z, z + 1 < line))
            def _():
                x_copy(s, k, UP).wait_send()

            @pl.when(jnp.logical_and(m >= z, z > 0))
            def _():
                x_copy(s, k, DOWN).wait_send()

        high_copy(s, mate).wait_send()

        @pl.when(s < away)
        def _():
            b_copy(s).wait_send()

        @pl.when(inside)
        def _():
            @pl.loop(0, n_row)
            def _(k):
                @pl.when(jnp.logical_not(jnp.logical_and(k == row, s >= away)))
                def _():
                    sw_copy(s, k).wait_send()

    for d in range(1, n_col):
        uv_copy(0, d, col).wait_send()
        uv_copy(1, d, col).wait_send()
    for h in range(subs):
        for d in range(1, n_row):
            g_copy(h, d, row).wait_send()


def shards(n_row, n_col, x_rhs, panel_u, panel_v, panel_rank, tile_p, tile_q, tile_rank):
    t_rows, t_cols, order, rank_cap = tile_p.shape
    x_rows, n_rhs = x_rhs.shape[1:]
    u_rows = panel_u.shape[1]
    width = n_rhs // n_col
    subs = 1
    part = width // subs
    steps = n_col * subs
    away = steps - subs
    fits = (
        n_rhs % n_col == 0
        and width % (128 * subs) == 0
        and x_rows % 16 == 0
        and u_rows % 128 == 0
        and n_row % 4 == 0
        and n_col > 1
        and n_col & (n_col - 1) == 0
        and t_cols % t_rows == 0
        and t_cols % 2 == 0
    )
    if not fits:
        return plain(x_rhs, panel_u, panel_v, panel_rank, tile_p, tile_q, tile_rank)
    dma = pltpu.SemaphoreType.DMA
    flops = 4 * order * rank_cap * n_rhs * t_rows * (t_cols + 1)
    return pl.pallas_call(
        functools.partial(kernel, n_row, n_col),
        out_shape=jax.ShapeDtypeStruct((t_rows, order, width), BF16),
        in_specs=[pl.BlockSpec(memory_space=pltpu.SMEM)] * 2
        + [pl.BlockSpec(memory_space=pl.ANY)] * 5,
        out_specs=pl.BlockSpec(memory_space=pltpu.VMEM),
        scratch_shapes=[
            pltpu.VMEM((steps, n_row, t_cols, x_rows, part), BF16),
            pltpu.VMEM(tile_p.shape, BF16),
            pltpu.VMEM(tile_q.shape, BF16),
            pltpu.VMEM((t_rows, t_cols, rank_cap, order), BF16),
            pltpu.VMEM((n_col, t_rows, u_rows, rank_cap), BF16),
            pltpu.VMEM((n_col, t_rows, u_rows, rank_cap), BF16),
            pltpu.VMEM((t_rows, rank_cap, order), BF16),
            pltpu.VMEM((t_rows, rank_cap, order), BF16),
            pltpu.VMEM((subs, t_rows, order, part), F32),
            pltpu.VMEM((order, part), F32),
            pltpu.VMEM((away, t_rows, order, part), BF16),
            pltpu.VMEM((away, t_rows, order, part), BF16),
            pltpu.VMEM((steps, n_row, x_rows, part), BF16),
            pltpu.VMEM((subs, n_row, x_rows, part), BF16),
            pltpu.VMEM((subs, n_row, x_rows, part), BF16),
            dma((steps, n_row, 3)),
            dma((steps, n_row)),
            dma((steps,)),
            dma((steps,)),
            dma((2, n_col)),
            dma((2, n_col)),
            dma((away,)),
            dma((away,)),
            dma((steps, n_row)),
            dma((subs, n_row)),
            dma((subs, n_row)),
            dma((subs, n_row)),
            dma((steps + 4,)),
        ],
        compiler_params=pltpu.CompilerParams(
            collective_id=0, has_side_effects=True, vmem_limit_bytes=56 * 2**20
        ),
        cost_estimate=pl.CostEstimate(flops=flops, bytes_accessed=20 * 2**20, transcendentals=0),
    )(tile_rank, panel_rank, x_rhs, panel_u, panel_v, tile_p, tile_q)


def solution(mesh):
    return jax.shard_map(
        functools.partial(shards, mesh.shape["row"], mesh.shape["col"]),
        mesh=mesh,
        in_specs=(
            P("col", "row", None),
            P("row", "col", None),
            P("row", "col", None),
            P(),
            P("row", "col", None, None),
            P("row", "col", None, None),
            P("row", "col"),
        ),
        out_specs=P("row", None, "col"),
        check_vma=False,
    )
```

```python
import functools

import jax
import jax.numpy as jnp
from jax import lax
from jax.experimental import pallas as pl
from jax.experimental.pallas import tpu as pltpu
from jax.sharding import PartitionSpec as P

BF16 = jnp.bfloat16
F32 = jnp.float32
MESH = pl.DeviceIdType.MESH
UP, DOWN, ACROSS = 0, 1, 2


def plain(x_rhs, panel_u, panel_v, panel_rank, tile_p, tile_q, tile_rank):
    exact = lax.Precision.HIGHEST
    row_at = lax.axis_index("row")
    col_at = lax.axis_index("col")
    t_rows = tile_p.shape[0]
    t_cols = tile_p.shape[1]
    rank_cap = tile_p.shape[3]
    gathered = lax.all_gather(x_rhs, "row", axis=1, tiled=True)
    full_u, full_v = (
        lax.all_gather(panel_u, "col", axis=1, tiled=True),
        lax.all_gather(panel_v, "col", axis=1, tiled=True),
    )
    tile_slot = lax.broadcasted_iota(jnp.int32, (1, 1, rank_cap, 1), 2)
    tile_proj = jnp.einsum("ijbr,jbn->ijrn", tile_q, gathered, preferred_element_type=jnp.float32)
    tile_proj = jnp.where(tile_slot < tile_rank[:, :, None, None], tile_proj, 0.0).astype(
        jnp.bfloat16
    )
    base_sum = jnp.einsum("ijbr,ijrn->ibn", tile_p, tile_proj, preferred_element_type=jnp.float32)
    rank_slot = lax.broadcasted_iota(jnp.int32, (1, rank_cap, 1), 1)
    row_rank = lax.dynamic_slice_in_dim(panel_rank, row_at * t_rows, t_rows)
    row_keep = rank_slot < row_rank[:, None, None]
    u_wide = full_u.astype(jnp.float32)
    tile_ids = row_at * t_rows + jnp.arange(t_rows, dtype=jnp.int32)
    inside = tile_ids // t_cols == col_at
    where_rhs = jnp.clip(tile_ids - col_at * t_cols, 0, t_cols - 1)
    picked = jnp.take(gathered, where_rhs, axis=0)
    keep = jnp.logical_and(inside[:, None, None], row_keep)
    panel_proj = jnp.einsum("jbr,jbn->jrn", full_u, picked, preferred_element_type=jnp.float32)
    panel_proj = jnp.where(keep, panel_proj, 0.0).astype(jnp.bfloat16)
    sweep_part = jnp.einsum("jbr,jrn->bn", full_v, panel_proj, preferred_element_type=jnp.float32)
    sweep_share = lax.psum_scatter(
        sweep_part.astype(jnp.bfloat16), "col", scatter_dimension=1, tiled=True
    )
    sweep = lax.psum(sweep_share, "row").astype(jnp.float32)
    back_proj = jnp.einsum("ibr,bn->irn", full_v.astype(jnp.float32), sweep, precision=exact)
    back_proj = jnp.where(row_keep, back_proj, 0.0)
    late_term = jnp.einsum("ibr,irn->ibn", u_wide, back_proj, precision=exact)
    summed = lax.psum_scatter(
        base_sum.astype(jnp.bfloat16), "col", scatter_dimension=2, tiled=True
    ).astype(jnp.float32)
    return (summed - late_term).astype(jnp.bfloat16)


def dot(a, b):
    return jnp.dot(a, b, preferred_element_type=F32)


def kernel(
    n_row, n_col,
    tile_rank, panel_rank, x_in, u_in, v_in, p_in, q_in,
    out,
    xg, pv, qv, qt, ug, vg, ut, vt, acc, sweep_acc, sbuf, rbuf, swb, swr, swg,
    x_send, x_recv, h_send, h_recv, uv_send, uv_recv, b_send, b_recv, sw_send, sw_recv, g_send, g_recv, local,
):
    t_rows, t_cols, order, rank_cap = pv.shape
    x_rows = xg.shape[3]
    width = xg.shape[4]
    u_rows = ug.shape[2]
    subs = swr.shape[0]
    steps = n_col * subs
    away = steps - subs
    ahead = 2
    half = t_cols // 2
    line = n_row // 2
    row = lax.axis_index("row")
    col = lax.axis_index("col")
    z, x = row // 2, row % 2
    mate = row + 1 - 2 * x
    odd = z % 2 == 1
    twin = row + 2 - 4 * (z % 2)
    inside = (row * t_rows) // t_cols == col
    first = lax.rem(row * t_rows, t_cols)

    def owner(s):
        flip = n_col - 1 - s // subs
        bits = [1 << b for b in range(n_col.bit_length() - 1)]
        return sum(lax.rem(col // b + flip // b, 2) * b for b in bits)

    def x_local(s):
        at = pl.multiple_of((owner(s) * subs + lax.rem(s, subs)) * width, width)
        return pltpu.make_async_copy(x_in.at[:, :, pl.ds(at, width)], xg.at[s, row], local.at[s])

    q_local = pltpu.make_async_copy(q_in, qv, local.at[steps])
    p_local = pltpu.make_async_copy(p_in, pv, local.at[steps + 1])
    u_local = pltpu.make_async_copy(u_in, ug.at[col], local.at[steps + 2])
    v_local = pltpu.make_async_copy(v_in, vg.at[col], local.at[steps + 3])
    x_local(0).start()
    u_local.start()
    v_local.start()
    for s in range(1, steps):
        x_local(s).start()
    q_local.start()
    p_local.start()

    barrier = pltpu.get_barrier_semaphore()

    @pl.loop(0, n_row * n_col)
    def _(k):
        @pl.when(k != row * n_col + col)
        def _():
            pl.semaphore_signal(
                barrier, inc=1, device_id=(k // n_col, lax.rem(k, n_col)), device_id_type=MESH
            )

    pl.semaphore_wait(barrier, n_row * n_col - 1)

    def x_copy(s, k, way):
        target = {UP: row + 2, DOWN: row - 2, ACROSS: mate}[way]
        return pltpu.make_async_remote_copy(
            src_ref=xg.at[s, k], dst_ref=xg.at[s, k],
            send_sem=x_send.at[s, k, way], recv_sem=x_recv.at[s, k],
            device_id=(target, col), device_id_type=MESH,
        )

    def low_copy(s, k):
        return pltpu.make_async_remote_copy(
            src_ref=xg.at[s, k, :half], dst_ref=xg.at[s, k, :half],
            send_sem=x_send.at[s, k, ACROSS], recv_sem=x_recv.at[s, k],
            device_id=(mate, col), device_id_type=MESH,
        )

    def high_copy(s, k):
        return pltpu.make_async_remote_copy(
            src_ref=xg.at[s, k, half:], dst_ref=xg.at[s, k, half:],
            send_sem=h_send.at[s], recv_sem=h_recv.at[s],
            device_id=(twin, col), device_id_type=MESH,
        )

    def across(s, k, is_twin):
        @pl.when(is_twin)
        def _():
            low_copy(s, k).start()

        @pl.when(jnp.logical_not(is_twin))
        def _():
            x_copy(s, k, ACROSS).start()

    def own_sends(s):
        x_local(s).wait()
        x_copy(s, row, ACROSS).start()

        @pl.when(z + 1 < line)
        def _():
            x_copy(s, row, UP).start()

        @pl.when(z > 0)
        def _():
            x_copy(s, row, DOWN).start()

    def forward(s, d):
        @pl.when(z - d >= 0)
        def _():
            k = row - 2 * d
            x_copy(s, k, ACROSS).wait_recv()
            across(s, k, odd) if d == 1 else x_copy(s, k, ACROSS).start()

            @pl.when(z + 1 < line)
            def _():
                x_copy(s, k, UP).start()

        @pl.when(z + d < line)
        def _():
            k = row + 2 * d
            x_copy(s, k, ACROSS).wait_recv()
            across(s, k, jnp.logical_not(odd)) if d == 1 else x_copy(s, k, ACROSS).start()

            @pl.when(z > 0)
            def _():
                x_copy(s, k, DOWN).start()

    def uv_copy(which, d, slot):
        ref = (ug, vg)[which]
        return pltpu.make_async_remote_copy(
            src_ref=ref.at[slot], dst_ref=ref.at[slot],
            send_sem=uv_send.at[which, d], recv_sem=uv_recv.at[which, d],
            device_id=(row, lax.rem(col + d, n_col)), device_id_type=MESH,
        )

    own_sends(0)
    u_local.wait()
    v_local.wait()
    for d in range(1, n_col):
        uv_copy(0, d, col).start()
        uv_copy(1, d, col).start()
    for s in range(1, ahead):
        own_sends(s)

    q_local.wait()

    @pl.loop(0, t_rows * t_cols)
    def _(k):
        i, j = k // t_cols, lax.rem(k, t_cols)
        keep = lax.broadcasted_iota(jnp.int32, (rank_cap, u_rows), 0) < tile_rank[i, j]
        for b in range(order // u_rows):
            at = pl.ds(b * u_rows, u_rows)
            qt[i, j, :, at] = jnp.where(keep, qv[i, j, at, :].T, jnp.zeros((), BF16))

    p_local.wait()
    for d in range(1, n_col):
        slot = lax.rem(col + n_col - d, n_col)
        uv_copy(0, d, slot).wait_recv()
        uv_copy(1, d, slot).wait_recv()

    @pl.loop(0, t_rows)
    def _(i):
        keep = (
            lax.broadcasted_iota(jnp.int32, (rank_cap, u_rows), 0) < panel_rank[row * t_rows + i]
        )
        for b in range(n_col):
            at = pl.ds(b * u_rows, u_rows)
            ut[i, :, at] = jnp.where(keep, ug[b, i].T, jnp.zeros((), BF16))
            vt[i, :, at] = jnp.where(keep, vg[b, i].T, jnp.zeros((), BF16))

    def b_copy(s):
        return pltpu.make_async_remote_copy(
            src_ref=sbuf.at[s], dst_ref=rbuf.at[s],
            send_sem=b_send.at[s], recv_sem=b_recv.at[s],
            device_id=(row, owner(s)), device_id_type=MESH,
        )

    def sw_copy(s, k):
        return pltpu.make_async_remote_copy(
            src_ref=swb.at[s, k], dst_ref=swr.at[lax.rem(s, subs), row],
            send_sem=sw_send.at[s, k], recv_sem=sw_recv.at[lax.rem(s, subs), row],
            device_id=(k, owner(s)), device_id_type=MESH,
        )

    def compute(s):
        low_copy(s, twin + 1 - 2 * x).wait_recv()
        high_copy(s, twin + 1 - 2 * x).wait_recv()
        for e in range(1, line // 2):
            pair = lax.rem(z // 2 + e, line // 2)
            for b in range(2):
                x_copy(s, 2 * (2 * pair + b) + 1 - x, ACROSS).wait_recv()

        @pl.when(inside)
        def _():
            for i in range(t_rows):
                block = xg[s, :, first + i].reshape(order, width)
                proj = dot(ut[i], block).astype(BF16)
                term = dot(vg[:, i].reshape(order, rank_cap), proj)
                if i == 0:
                    sweep_acc[...] = term
                else:
                    sweep_acc[...] += term
            swb[s] = sweep_acc[...].astype(BF16).reshape(n_row, x_rows, width)

            @pl.loop(0, n_row)
            def _(k):
                mine = jnp.logical_and(k == row, s >= away)

                @pl.when(mine)
                def _():
                    swr[s - away, row] = swb[s, row]

                @pl.when(jnp.logical_not(mine))
                def _():
                    sw_copy(s, k).start()

        @pl.loop(0, t_rows)
        def _(i):
            total = None
            for j in range(t_cols):
                proj = dot(qt[i, j], xg[s, :, j].reshape(order, width)).astype(BF16)
                term = dot(pv[i, j], proj)
                total = term if total is None else total + term

            @pl.when(s < away)
            def _():
                sbuf[s, i] = total.astype(BF16)

            @pl.when(s >= away)
            def _():
                acc[lax.rem(s, subs), i] = total

        @pl.when(s < away)
        def _():
            b_copy(s).start()

    def reduce_sweep(h):
        for k in range(n_row):
            @pl.when(jnp.logical_not(jnp.logical_and(inside, k == row)))
            def _():
                pltpu.make_async_remote_copy(
                    src_ref=swr.at[h, k], dst_ref=swr.at[h, k],
                    send_sem=sw_send.at[h, k], recv_sem=sw_recv.at[h, k],
                    device_id=(row, col), device_id_type=MESH,
                ).wait_recv()

        total = swr[h, 0].astype(F32)
        for k in range(1, n_row):
            total = total + swr[h, k].astype(F32)
        swg[h, row] = total.astype(BF16)
        for e in range(1, line):
            g_along(h, e, row).start()
        g_across(h, 0, row).start()

    def g_along(h, e, slot):
        return pltpu.make_async_remote_copy(
            src_ref=swg.at[h, slot], dst_ref=swg.at[h, slot],
            send_sem=g_send.at[h, e], recv_sem=g_recv.at[h, slot],
            device_id=(2 * lax.rem(z + e, line) + x, col), device_id_type=MESH,
        )

    def g_across(h, e, slot):
        return pltpu.make_async_remote_copy(
            src_ref=swg.at[h, slot], dst_ref=swg.at[h, slot],
            send_sem=g_send.at[h, line + e], recv_sem=g_recv.at[h, slot],
            device_id=(mate, col), device_id_type=MESH,
        )

    def relay_sweep(h):
        for e in range(1, line):
            slot = 2 * lax.rem(z + line - e, line) + x
            g_along(h, e, slot).wait_recv()
            g_across(h, e, slot).start()

    def add_received(h):
        for g in range(n_col - 1):
            b_copy(g * subs + h).wait_recv()

        @pl.loop(0, t_rows)
        def _(i):
            total = acc[h, i]
            for g in range(n_col - 1):
                total = total + rbuf[g * subs + h, i].astype(F32)
            acc[h, i] = total

    def finish(h):
        for e in range(line):
            g_across(h, e, 2 * lax.rem(z + e, line) + 1 - x).wait_recv()

        @pl.loop(0, t_rows)
        def _(i):
            back = dot(vt[i], swg[h].reshape(order, width)).astype(BF16)
            late = dot(ug[:, i].reshape(order, rank_cap), back)
            out[i, :, h * width : (h + 1) * width] = (acc[h, i] - late).astype(BF16)

    @pl.loop(0, steps + 1)
    def _(s):
        @pl.when(s < steps)
        def _():
            forward(s, 1)
            x_copy(s, mate, ACROSS).wait_recv()
            high_copy(s, mate).start()

        @pl.when(s + ahead < steps)
        def _():
            own_sends(s + ahead)

        @pl.when(s == steps)
        def _():
            for h in range(subs - 1):
                reduce_sweep(h)

        @pl.when(s < steps)
        def _():
            for d in range(2, line):
                forward(s, d)

        @pl.when(s > 0)
        def _():
            compute(s - 1)

    reduce_sweep(subs - 1)
    for h in range(subs):
        add_received(h)
    for h in range(subs):
        relay_sweep(h)
    for h in range(subs):
        finish(h)

    @pl.loop(0, steps)
    def _(s):
        for m in range(line):
            k = 2 * m + x
            @pl.when(k == twin)
            def _():
                low_copy(s, k).wait_send()

            @pl.when(k != twin)
            def _():
                x_copy(s, k, ACROSS).wait_send()

            @pl.when(jnp.logical_and(m <= z, z + 1 < line))
            def _():
                x_copy(s, k, UP).wait_send()

            @pl.when(jnp.logical_and(m >= z, z > 0))
            def _():
                x_copy(s, k, DOWN).wait_send()

        high_copy(s, mate).wait_send()

        @pl.when(s < away)
        def _():
            b_copy(s).wait_send()

        @pl.when(inside)
        def _():
            @pl.loop(0, n_row)
            def _(k):
                @pl.when(jnp.logical_not(jnp.logical_and(k == row, s >= away)))
                def _():
                    sw_copy(s, k).wait_send()

    for d in range(1, n_col):
        uv_copy(0, d, col).wait_send()
        uv_copy(1, d, col).wait_send()
    for h in range(subs):
        for e in range(line):
            if e > 0:
                g_along(h, e, row).wait_send()
            g_across(h, e, row).wait_send()


def shards(n_row, n_col, x_rhs, panel_u, panel_v, panel_rank, tile_p, tile_q, tile_rank):
    t_rows, t_cols, order, rank_cap = tile_p.shape
    x_rows, n_rhs = x_rhs.shape[1:]
    u_rows = panel_u.shape[1]
    width = n_rhs // n_col
    subs = 1
    part = width // subs
    steps = n_col * subs
    away = steps - subs
    fits = (
        n_rhs % n_col == 0
        and width % (128 * subs) == 0
        and x_rows % 16 == 0
        and u_rows % 128 == 0
        and n_row % 4 == 0
        and n_col > 1
        and n_col & (n_col - 1) == 0
        and t_cols % t_rows == 0
        and t_cols % 2 == 0
    )
    if not fits:
        return plain(x_rhs, panel_u, panel_v, panel_rank, tile_p, tile_q, tile_rank)
    dma = pltpu.SemaphoreType.DMA
    flops = 4 * order * rank_cap * n_rhs * t_rows * (t_cols + 1)
    return pl.pallas_call(
        functools.partial(kernel, n_row, n_col),
        out_shape=jax.ShapeDtypeStruct((t_rows, order, width), BF16),
        in_specs=[pl.BlockSpec(memory_space=pltpu.SMEM)] * 2
        + [pl.BlockSpec(memory_space=pl.ANY)] * 5,
        out_specs=pl.BlockSpec(memory_space=pltpu.VMEM),
        scratch_shapes=[
            pltpu.VMEM((steps, n_row, t_cols, x_rows, part), BF16),
            pltpu.VMEM(tile_p.shape, BF16),
            pltpu.VMEM(tile_q.shape, BF16),
            pltpu.VMEM((t_rows, t_cols, rank_cap, order), BF16),
            pltpu.VMEM((n_col, t_rows, u_rows, rank_cap), BF16),
            pltpu.VMEM((n_col, t_rows, u_rows, rank_cap), BF16),
            pltpu.VMEM((t_rows, rank_cap, order), BF16),
            pltpu.VMEM((t_rows, rank_cap, order), BF16),
            pltpu.VMEM((subs, t_rows, order, part), F32),
            pltpu.VMEM((order, part), F32),
            pltpu.VMEM((away, t_rows, order, part), BF16),
            pltpu.VMEM((away, t_rows, order, part), BF16),
            pltpu.VMEM((steps, n_row, x_rows, part), BF16),
            pltpu.VMEM((subs, n_row, x_rows, part), BF16),
            pltpu.VMEM((subs, n_row, x_rows, part), BF16),
            dma((steps, n_row, 3)),
            dma((steps, n_row)),
            dma((steps,)),
            dma((steps,)),
            dma((2, n_col)),
            dma((2, n_col)),
            dma((away,)),
            dma((away,)),
            dma((steps, n_row)),
            dma((subs, n_row)),
            dma((subs, n_row)),
            dma((subs, n_row)),
            dma((steps + 4,)),
        ],
        compiler_params=pltpu.CompilerParams(
            collective_id=0, has_side_effects=True, vmem_limit_bytes=56 * 2**20
        ),
        cost_estimate=pl.CostEstimate(flops=flops, bytes_accessed=20 * 2**20, transcendentals=0),
    )(tile_rank, panel_rank, x_rhs, panel_u, panel_v, tile_p, tile_q)


def solution(mesh):
    return jax.shard_map(
        functools.partial(shards, mesh.shape["row"], mesh.shape["col"]),
        mesh=mesh,
        in_specs=(
            P("col", "row", None),
            P("row", "col", None),
            P("row", "col", None),
            P(),
            P("row", "col", None, None),
            P("row", "col", None, None),
            P("row", "col"),
        ),
        out_specs=P("row", None, "col"),
        check_vma=False,
    )
```

```python
import functools

import jax
import jax.numpy as jnp
from jax import lax
from jax.experimental import pallas as pl
from jax.experimental.pallas import tpu as pltpu
from jax.sharding import PartitionSpec as P

BF16 = jnp.bfloat16
F32 = jnp.float32
MESH = pl.DeviceIdType.MESH
UP, DOWN, ACROSS = 0, 1, 2


def plain(x_rhs, panel_u, panel_v, panel_rank, tile_p, tile_q, tile_rank):
    exact = lax.Precision.HIGHEST
    row_at = lax.axis_index("row")
    col_at = lax.axis_index("col")
    t_rows = tile_p.shape[0]
    t_cols = tile_p.shape[1]
    rank_cap = tile_p.shape[3]
    gathered = lax.all_gather(x_rhs, "row", axis=1, tiled=True)
    full_u, full_v = (
        lax.all_gather(panel_u, "col", axis=1, tiled=True),
        lax.all_gather(panel_v, "col", axis=1, tiled=True),
    )
    tile_slot = lax.broadcasted_iota(jnp.int32, (1, 1, rank_cap, 1), 2)
    tile_proj = jnp.einsum("ijbr,jbn->ijrn", tile_q, gathered, preferred_element_type=jnp.float32)
    tile_proj = jnp.where(tile_slot < tile_rank[:, :, None, None], tile_proj, 0.0).astype(
        jnp.bfloat16
    )
    base_sum = jnp.einsum("ijbr,ijrn->ibn", tile_p, tile_proj, preferred_element_type=jnp.float32)
    rank_slot = lax.broadcasted_iota(jnp.int32, (1, rank_cap, 1), 1)
    row_rank = lax.dynamic_slice_in_dim(panel_rank, row_at * t_rows, t_rows)
    row_keep = rank_slot < row_rank[:, None, None]
    u_wide = full_u.astype(jnp.float32)
    tile_ids = row_at * t_rows + jnp.arange(t_rows, dtype=jnp.int32)
    inside = tile_ids // t_cols == col_at
    where_rhs = jnp.clip(tile_ids - col_at * t_cols, 0, t_cols - 1)
    picked = jnp.take(gathered, where_rhs, axis=0)
    keep = jnp.logical_and(inside[:, None, None], row_keep)
    panel_proj = jnp.einsum("jbr,jbn->jrn", full_u, picked, preferred_element_type=jnp.float32)
    panel_proj = jnp.where(keep, panel_proj, 0.0).astype(jnp.bfloat16)
    sweep_part = jnp.einsum("jbr,jrn->bn", full_v, panel_proj, preferred_element_type=jnp.float32)
    sweep_share = lax.psum_scatter(
        sweep_part.astype(jnp.bfloat16), "col", scatter_dimension=1, tiled=True
    )
    sweep = lax.psum(sweep_share, "row").astype(jnp.float32)
    back_proj = jnp.einsum("ibr,bn->irn", full_v.astype(jnp.float32), sweep, precision=exact)
    back_proj = jnp.where(row_keep, back_proj, 0.0)
    late_term = jnp.einsum("ibr,irn->ibn", u_wide, back_proj, precision=exact)
    summed = lax.psum_scatter(
        base_sum.astype(jnp.bfloat16), "col", scatter_dimension=2, tiled=True
    ).astype(jnp.float32)
    return (summed - late_term).astype(jnp.bfloat16)


def dot(a, b):
    return jnp.dot(a, b, preferred_element_type=F32)


def kernel(
    n_row, n_col,
    tile_rank, panel_rank, x_in, u_in, v_in, p_in, q_in,
    out,
    xg, pv, qv, qt, ug, vg, ut, vt, acc, sweep_acc, sbuf, rbuf, swb, swr, swg,
    x_send, x_recv, h_send, h_recv, uv_send, uv_recv, b_send, b_recv, sw_send, sw_recv, g_send, g_recv, local,
):
    t_rows, t_cols, order, rank_cap = pv.shape
    x_rows = xg.shape[3]
    width = xg.shape[4]
    u_rows = ug.shape[2]
    subs = swr.shape[0]
    steps = n_col * subs
    away = steps - subs
    ahead = 2 * subs
    half = t_cols // 2
    line = n_row // 2
    row = lax.axis_index("row")
    col = lax.axis_index("col")
    z, x = row // 2, row % 2
    mate = row + 1 - 2 * x
    odd = z % 2 == 1
    twin = row + 2 - 4 * (z % 2)
    inside = (row * t_rows) // t_cols == col
    first = lax.rem(row * t_rows, t_cols)

    def owner(s):
        flip = n_col - 1 - s // subs
        bits = [1 << b for b in range(n_col.bit_length() - 1)]
        return sum(lax.rem(col // b + flip // b, 2) * b for b in bits)

    def x_local(s):
        at = pl.multiple_of((owner(s) * subs + lax.rem(s, subs)) * width, width)
        return pltpu.make_async_copy(x_in.at[:, :, pl.ds(at, width)], xg.at[s, row], local.at[s])

    q_local = pltpu.make_async_copy(q_in, qv, local.at[steps])
    p_local = pltpu.make_async_copy(p_in, pv, local.at[steps + 1])
    u_local = pltpu.make_async_copy(u_in, ug.at[col], local.at[steps + 2])
    v_local = pltpu.make_async_copy(v_in, vg.at[col], local.at[steps + 3])
    x_local(0).start()
    u_local.start()
    v_local.start()
    for s in range(1, steps):
        x_local(s).start()
    q_local.start()
    p_local.start()

    barrier = pltpu.get_barrier_semaphore()

    @pl.loop(0, n_row * n_col)
    def _(k):
        @pl.when(k != row * n_col + col)
        def _():
            pl.semaphore_signal(
                barrier, inc=1, device_id=(k // n_col, lax.rem(k, n_col)), device_id_type=MESH
            )

    pl.semaphore_wait(barrier, n_row * n_col - 1)

    def x_copy(s, k, way):
        target = {UP: row + 2, DOWN: row - 2, ACROSS: mate}[way]
        return pltpu.make_async_remote_copy(
            src_ref=xg.at[s, k], dst_ref=xg.at[s, k],
            send_sem=x_send.at[s, k, way], recv_sem=x_recv.at[s, k],
            device_id=(target, col), device_id_type=MESH,
        )

    def low_copy(s, k):
        return pltpu.make_async_remote_copy(
            src_ref=xg.at[s, k, :half], dst_ref=xg.at[s, k, :half],
            send_sem=x_send.at[s, k, ACROSS], recv_sem=x_recv.at[s, k],
            device_id=(mate, col), device_id_type=MESH,
        )

    def high_copy(s, k):
        return pltpu.make_async_remote_copy(
            src_ref=xg.at[s, k, half:], dst_ref=xg.at[s, k, half:],
            send_sem=h_send.at[s], recv_sem=h_recv.at[s],
            device_id=(twin, col), device_id_type=MESH,
        )

    def across(s, k, is_twin):
        @pl.when(is_twin)
        def _():
            low_copy(s, k).start()

        @pl.when(jnp.logical_not(is_twin))
        def _():
            x_copy(s, k, ACROSS).start()

    def own_sends(s):
        x_local(s).wait()
        x_copy(s, row, ACROSS).start()

        @pl.when(z + 1 < line)
        def _():
            x_copy(s, row, UP).start()

        @pl.when(z > 0)
        def _():
            x_copy(s, row, DOWN).start()

    def forward(s, d):
        @pl.when(z - d >= 0)
        def _():
            k = row - 2 * d
            x_copy(s, k, ACROSS).wait_recv()
            across(s, k, odd) if d == 1 else x_copy(s, k, ACROSS).start()

            @pl.when(z + 1 < line)
            def _():
                x_copy(s, k, UP).start()

        @pl.when(z + d < line)
        def _():
            k = row + 2 * d
            x_copy(s, k, ACROSS).wait_recv()
            across(s, k, jnp.logical_not(odd)) if d == 1 else x_copy(s, k, ACROSS).start()

            @pl.when(z > 0)
            def _():
                x_copy(s, k, DOWN).start()

    def uv_copy(which, d, slot):
        ref = (ug, vg)[which]
        return pltpu.make_async_remote_copy(
            src_ref=ref.at[slot], dst_ref=ref.at[slot],
            send_sem=uv_send.at[which, d], recv_sem=uv_recv.at[which, d],
            device_id=(row, lax.rem(col + d, n_col)), device_id_type=MESH,
        )

    own_sends(0)
    u_local.wait()
    v_local.wait()
    for d in range(1, n_col):
        uv_copy(0, d, col).start()
        uv_copy(1, d, col).start()
    for s in range(1, ahead):
        own_sends(s)

    q_local.wait()

    @pl.loop(0, t_rows * t_cols)
    def _(k):
        i, j = k // t_cols, lax.rem(k, t_cols)
        keep = lax.broadcasted_iota(jnp.int32, (rank_cap, u_rows), 0) < tile_rank[i, j]
        for b in range(order // u_rows):
            at = pl.ds(b * u_rows, u_rows)
            qt[i, j, :, at] = jnp.where(keep, qv[i, j, at, :].T, jnp.zeros((), BF16))

    p_local.wait()
    for d in range(1, n_col):
        slot = lax.rem(col + n_col - d, n_col)
        uv_copy(0, d, slot).wait_recv()
        uv_copy(1, d, slot).wait_recv()

    @pl.loop(0, t_rows)
    def _(i):
        keep = (
            lax.broadcasted_iota(jnp.int32, (rank_cap, u_rows), 0) < panel_rank[row * t_rows + i]
        )
        for b in range(n_col):
            at = pl.ds(b * u_rows, u_rows)
            ut[i, :, at] = jnp.where(keep, ug[b, i].T, jnp.zeros((), BF16))
            vt[i, :, at] = jnp.where(keep, vg[b, i].T, jnp.zeros((), BF16))

    def b_copy(s):
        return pltpu.make_async_remote_copy(
            src_ref=sbuf.at[s], dst_ref=rbuf.at[s],
            send_sem=b_send.at[s], recv_sem=b_recv.at[s],
            device_id=(row, owner(s)), device_id_type=MESH,
        )

    def sw_copy(s, k):
        return pltpu.make_async_remote_copy(
            src_ref=swb.at[s, k], dst_ref=swr.at[lax.rem(s, subs), row],
            send_sem=sw_send.at[s, k], recv_sem=sw_recv.at[lax.rem(s, subs), row],
            device_id=(k, owner(s)), device_id_type=MESH,
        )

    def compute(span, own):
        wide = len(span) * width

        def block(j):
            parts = [xg[s, :, j].reshape(order, width) for s in span]
            return parts[0] if len(parts) == 1 else jnp.concatenate(parts, axis=1)

        for s in span:
            low_copy(s, twin + 1 - 2 * x).wait_recv()
            high_copy(s, twin + 1 - 2 * x).wait_recv()
            for e in range(1, line // 2):
                pair = lax.rem(z // 2 + e, line // 2)
                for b in range(2):
                    x_copy(s, 2 * (2 * pair + b) + 1 - x, ACROSS).wait_recv()

        @pl.when(inside)
        def _():
            for i in range(t_rows):
                proj = dot(ut[i], block(first + i)).astype(BF16)
                term = dot(vg[:, i].reshape(order, rank_cap), proj)
                if i == 0:
                    sweep_acc[:, :wide] = term
                else:
                    sweep_acc[:, :wide] += term
            for n, s in enumerate(span):
                cut = sweep_acc[:, n * width : (n + 1) * width]
                swb[s] = cut.astype(BF16).reshape(n_row, x_rows, width)

                @pl.loop(0, n_row)
                def _(k):
                    if own:
                        @pl.when(k == row)
                        def _():
                            swr[s - away, row] = swb[s, row]

                        @pl.when(k != row)
                        def _():
                            sw_copy(s, k).start()
                    else:
                        sw_copy(s, k).start()

        @pl.loop(0, t_rows)
        def _(i):
            total = None
            for j in range(t_cols):
                proj = dot(qt[i, j], block(j)).astype(BF16)
                term = dot(pv[i, j], proj)
                total = term if total is None else total + term

            for n, s in enumerate(span):
                cut = total[:, n * width : (n + 1) * width]
                if own:
                    acc[s - away, i] = cut
                else:
                    sbuf[s, i] = cut.astype(BF16)

        if not own:
            for s in span:
                b_copy(s).start()

    def reduce_sweep(h):
        for k in range(n_row):
            @pl.when(jnp.logical_not(jnp.logical_and(inside, k == row)))
            def _():
                pltpu.make_async_remote_copy(
                    src_ref=swr.at[h, k], dst_ref=swr.at[h, k],
                    send_sem=sw_send.at[h, k], recv_sem=sw_recv.at[h, k],
                    device_id=(row, col), device_id_type=MESH,
                ).wait_recv()

        total = swr[h, 0].astype(F32)
        for k in range(1, n_row):
            total = total + swr[h, k].astype(F32)
        swg[h, row] = total.astype(BF16)
        for e in range(1, line):
            g_along(h, e, row).start()
        g_across(h, 0, row).start()

    def g_along(h, e, slot):
        return pltpu.make_async_remote_copy(
            src_ref=swg.at[h, slot], dst_ref=swg.at[h, slot],
            send_sem=g_send.at[h, e], recv_sem=g_recv.at[h, slot],
            device_id=(2 * lax.rem(z + e, line) + x, col), device_id_type=MESH,
        )

    def g_across(h, e, slot):
        return pltpu.make_async_remote_copy(
            src_ref=swg.at[h, slot], dst_ref=swg.at[h, slot],
            send_sem=g_send.at[h, line + e], recv_sem=g_recv.at[h, slot],
            device_id=(mate, col), device_id_type=MESH,
        )

    def relay_sweep(h):
        for e in range(1, line):
            slot = 2 * lax.rem(z + line - e, line) + x
            g_along(h, e, slot).wait_recv()
            g_across(h, e, slot).start()

    def add_received(h):
        for g in range(n_col - 1):
            b_copy(g * subs + h).wait_recv()

        @pl.loop(0, t_rows)
        def _(i):
            total = acc[h, i]
            for g in range(n_col - 1):
                total = total + rbuf[g * subs + h, i].astype(F32)
            acc[h, i] = total

    def finish(h):
        for e in range(line):
            g_across(h, e, 2 * lax.rem(z + e, line) + 1 - x).wait_recv()

        @pl.loop(0, t_rows)
        def _(i):
            back = dot(vt[i], swg[h].reshape(order, width)).astype(BF16)
            late = dot(ug[:, i].reshape(order, rank_cap), back)
            out[i, :, h * width : (h + 1) * width] = (acc[h, i] - late).astype(BF16)

    @pl.loop(0, steps + 1)
    def _(s):
        @pl.when(s < steps)
        def _():
            forward(s, 1)
            x_copy(s, mate, ACROSS).wait_recv()
            high_copy(s, mate).start()

        @pl.when(s + ahead < steps)
        def _():
            own_sends(s + ahead)

        @pl.when(s == steps)
        def _():
            for h in range(subs - 1):
                reduce_sweep(h)

        @pl.when(s < steps)
        def _():
            for d in range(2, line):
                forward(s, d)

        @pl.when(jnp.logical_and(jnp.logical_and(s > 0, s <= away), lax.rem(s, subs) == 0))
        def _():
            compute([s - subs + h for h in range(subs)], False)

        @pl.when(s > away)
        def _():
            compute([s - 1], True)

    reduce_sweep(subs - 1)
    for h in range(subs):
        add_received(h)
    for h in range(subs):
        relay_sweep(h)
    for h in range(subs):
        finish(h)

    @pl.loop(0, steps)
    def _(s):
        for m in range(line):
            k = 2 * m + x
            @pl.when(k == twin)
            def _():
                low_copy(s, k).wait_send()

            @pl.when(k != twin)
            def _():
                x_copy(s, k, ACROSS).wait_send()

            @pl.when(jnp.logical_and(m <= z, z + 1 < line))
            def _():
                x_copy(s, k, UP).wait_send()

            @pl.when(jnp.logical_and(m >= z, z > 0))
            def _():
                x_copy(s, k, DOWN).wait_send()

        high_copy(s, mate).wait_send()

        @pl.when(s < away)
        def _():
            b_copy(s).wait_send()

        @pl.when(inside)
        def _():
            @pl.loop(0, n_row)
            def _(k):
                @pl.when(jnp.logical_not(jnp.logical_and(k == row, s >= away)))
                def _():
                    sw_copy(s, k).wait_send()

    for d in range(1, n_col):
        uv_copy(0, d, col).wait_send()
        uv_copy(1, d, col).wait_send()
    for h in range(subs):
        for e in range(line):
            if e > 0:
                g_along(h, e, row).wait_send()
            g_across(h, e, row).wait_send()


def shards(n_row, n_col, x_rhs, panel_u, panel_v, panel_rank, tile_p, tile_q, tile_rank):
    t_rows, t_cols, order, rank_cap = tile_p.shape
    x_rows, n_rhs = x_rhs.shape[1:]
    u_rows = panel_u.shape[1]
    width = n_rhs // n_col
    subs = 2
    part = width // subs
    steps = n_col * subs
    away = steps - subs
    fits = (
        n_rhs % n_col == 0
        and width % (128 * subs) == 0
        and x_rows % 16 == 0
        and u_rows % 128 == 0
        and n_row % 4 == 0
        and n_col > 1
        and n_col & (n_col - 1) == 0
        and t_cols % t_rows == 0
        and t_cols % 2 == 0
    )
    if not fits:
        return plain(x_rhs, panel_u, panel_v, panel_rank, tile_p, tile_q, tile_rank)
    dma = pltpu.SemaphoreType.DMA
    flops = 4 * order * rank_cap * n_rhs * t_rows * (t_cols + 1)
    return pl.pallas_call(
        functools.partial(kernel, n_row, n_col),
        out_shape=jax.ShapeDtypeStruct((t_rows, order, width), BF16),
        in_specs=[pl.BlockSpec(memory_space=pltpu.SMEM)] * 2
        + [pl.BlockSpec(memory_space=pl.ANY)] * 5,
        out_specs=pl.BlockSpec(memory_space=pltpu.VMEM),
        scratch_shapes=[
            pltpu.VMEM((steps, n_row, t_cols, x_rows, part), BF16),
            pltpu.VMEM(tile_p.shape, BF16),
            pltpu.VMEM(tile_q.shape, BF16),
            pltpu.VMEM((t_rows, t_cols, rank_cap, order), BF16),
            pltpu.VMEM((n_col, t_rows, u_rows, rank_cap), BF16),
            pltpu.VMEM((n_col, t_rows, u_rows, rank_cap), BF16),
            pltpu.VMEM((t_rows, rank_cap, order), BF16),
            pltpu.VMEM((t_rows, rank_cap, order), BF16),
            pltpu.VMEM((subs, t_rows, order, part), F32),
            pltpu.VMEM((order, width), F32),
            pltpu.VMEM((away, t_rows, order, part), BF16),
            pltpu.VMEM((away, t_rows, order, part), BF16),
            pltpu.VMEM((steps, n_row, x_rows, part), BF16),
            pltpu.VMEM((subs, n_row, x_rows, part), BF16),
            pltpu.VMEM((subs, n_row, x_rows, part), BF16),
            dma((steps, n_row, 3)),
            dma((steps, n_row)),
            dma((steps,)),
            dma((steps,)),
            dma((2, n_col)),
            dma((2, n_col)),
            dma((away,)),
            dma((away,)),
            dma((steps, n_row)),
            dma((subs, n_row)),
            dma((subs, n_row)),
            dma((subs, n_row)),
            dma((steps + 4,)),
        ],
        compiler_params=pltpu.CompilerParams(
            collective_id=0, has_side_effects=True, vmem_limit_bytes=56 * 2**20
        ),
        cost_estimate=pl.CostEstimate(flops=flops, bytes_accessed=20 * 2**20, transcendentals=0),
    )(tile_rank, panel_rank, x_rhs, panel_u, panel_v, tile_p, tile_q)


def solution(mesh):
    return jax.shard_map(
        functools.partial(shards, mesh.shape["row"], mesh.shape["col"]),
        mesh=mesh,
        in_specs=(
            P("col", "row", None),
            P("row", "col", None),
            P("row", "col", None),
            P(),
            P("row", "col", None, None),
            P("row", "col", None, None),
            P("row", "col"),
        ),
        out_specs=P("row", None, "col"),
        check_vma=False,
    )
```

```python
import functools

import jax
import jax.numpy as jnp
from jax import lax
from jax.experimental import pallas as pl
from jax.experimental.pallas import tpu as pltpu
from jax.sharding import PartitionSpec as P

BF16 = jnp.bfloat16
F32 = jnp.float32
MESH = pl.DeviceIdType.MESH
UP, DOWN, ACROSS = 0, 1, 2


def plain(x_rhs, panel_u, panel_v, panel_rank, tile_p, tile_q, tile_rank):
    exact = lax.Precision.HIGHEST
    row_at = lax.axis_index("row")
    col_at = lax.axis_index("col")
    t_rows = tile_p.shape[0]
    t_cols = tile_p.shape[1]
    rank_cap = tile_p.shape[3]
    gathered = lax.all_gather(x_rhs, "row", axis=1, tiled=True)
    full_u, full_v = (
        lax.all_gather(panel_u, "col", axis=1, tiled=True),
        lax.all_gather(panel_v, "col", axis=1, tiled=True),
    )
    tile_slot = lax.broadcasted_iota(jnp.int32, (1, 1, rank_cap, 1), 2)
    tile_proj = jnp.einsum("ijbr,jbn->ijrn", tile_q, gathered, preferred_element_type=jnp.float32)
    tile_proj = jnp.where(tile_slot < tile_rank[:, :, None, None], tile_proj, 0.0).astype(
        jnp.bfloat16
    )
    base_sum = jnp.einsum("ijbr,ijrn->ibn", tile_p, tile_proj, preferred_element_type=jnp.float32)
    rank_slot = lax.broadcasted_iota(jnp.int32, (1, rank_cap, 1), 1)
    row_rank = lax.dynamic_slice_in_dim(panel_rank, row_at * t_rows, t_rows)
    row_keep = rank_slot < row_rank[:, None, None]
    u_wide = full_u.astype(jnp.float32)
    tile_ids = row_at * t_rows + jnp.arange(t_rows, dtype=jnp.int32)
    inside = tile_ids // t_cols == col_at
    where_rhs = jnp.clip(tile_ids - col_at * t_cols, 0, t_cols - 1)
    picked = jnp.take(gathered, where_rhs, axis=0)
    keep = jnp.logical_and(inside[:, None, None], row_keep)
    panel_proj = jnp.einsum("jbr,jbn->jrn", full_u, picked, preferred_element_type=jnp.float32)
    panel_proj = jnp.where(keep, panel_proj, 0.0).astype(jnp.bfloat16)
    sweep_part = jnp.einsum("jbr,jrn->bn", full_v, panel_proj, preferred_element_type=jnp.float32)
    sweep_share = lax.psum_scatter(
        sweep_part.astype(jnp.bfloat16), "col", scatter_dimension=1, tiled=True
    )
    sweep = lax.psum(sweep_share, "row").astype(jnp.float32)
    back_proj = jnp.einsum("ibr,bn->irn", full_v.astype(jnp.float32), sweep, precision=exact)
    back_proj = jnp.where(row_keep, back_proj, 0.0)
    late_term = jnp.einsum("ibr,irn->ibn", u_wide, back_proj, precision=exact)
    summed = lax.psum_scatter(
        base_sum.astype(jnp.bfloat16), "col", scatter_dimension=2, tiled=True
    ).astype(jnp.float32)
    return (summed - late_term).astype(jnp.bfloat16)


def dot(a, b):
    return jnp.dot(a, b, preferred_element_type=F32)


def kernel(
    n_row, n_col,
    tile_rank, panel_rank, x_in, u_in, v_in, p_in, q_in,
    out,
    xg, pv, qv, qt, ug, vg, ut, vt, acc, sweep_acc, sbuf, rbuf, swb, swr, swg,
    x_send, x_recv, h_send, h_recv, uv_send, uv_recv, b_send, b_recv, sw_send, sw_recv, g_send, g_recv, local,
):
    t_rows, t_cols, order, rank_cap = pv.shape
    x_rows = xg.shape[3]
    width = xg.shape[4]
    u_rows = ug.shape[2]
    subs = swr.shape[0]
    steps = n_col * subs
    away = steps - subs
    ahead = 2
    half = t_cols // 2
    line = n_row // 2
    row = lax.axis_index("row")
    col = lax.axis_index("col")
    z, x = row // 2, row % 2
    mate = row + 1 - 2 * x
    odd = z % 2 == 1
    twin = row + 2 - 4 * (z % 2)
    inside = (row * t_rows) // t_cols == col
    first = lax.rem(row * t_rows, t_cols)

    def owner(s):
        flip = n_col - 1 - s // subs
        bits = [1 << b for b in range(n_col.bit_length() - 1)]
        return sum(lax.rem(col // b + flip // b, 2) * b for b in bits)

    def x_local(s):
        at = pl.multiple_of((owner(s) * subs + lax.rem(s, subs)) * width, width)
        return pltpu.make_async_copy(x_in.at[:, :, pl.ds(at, width)], xg.at[s, row], local.at[s])

    q_local = pltpu.make_async_copy(q_in, qv, local.at[steps])
    p_local = pltpu.make_async_copy(p_in, pv, local.at[steps + 1])
    u_local = pltpu.make_async_copy(u_in, ug.at[col], local.at[steps + 2])
    v_local = pltpu.make_async_copy(v_in, vg.at[col], local.at[steps + 3])
    x_local(0).start()
    u_local.start()
    v_local.start()
    for s in range(1, steps):
        x_local(s).start()
    q_local.start()
    p_local.start()

    barrier = pltpu.get_barrier_semaphore()

    @pl.loop(0, n_row * n_col)
    def _(k):
        @pl.when(k != row * n_col + col)
        def _():
            pl.semaphore_signal(
                barrier, inc=1, device_id=(k // n_col, lax.rem(k, n_col)), device_id_type=MESH
            )

    pl.semaphore_wait(barrier, n_row * n_col - 1)

    def x_copy(s, k, way):
        target = {UP: row + 2, DOWN: row - 2, ACROSS: mate}[way]
        return pltpu.make_async_remote_copy(
            src_ref=xg.at[s, k], dst_ref=xg.at[s, k],
            send_sem=x_send.at[s, k, way], recv_sem=x_recv.at[s, k],
            device_id=(target, col), device_id_type=MESH,
        )

    def low_copy(s, k):
        return pltpu.make_async_remote_copy(
            src_ref=xg.at[s, k, :half], dst_ref=xg.at[s, k, :half],
            send_sem=x_send.at[s, k, ACROSS], recv_sem=x_recv.at[s, k],
            device_id=(mate, col), device_id_type=MESH,
        )

    def high_copy(s, k):
        return pltpu.make_async_remote_copy(
            src_ref=xg.at[s, k, half:], dst_ref=xg.at[s, k, half:],
            send_sem=h_send.at[s], recv_sem=h_recv.at[s],
            device_id=(twin, col), device_id_type=MESH,
        )

    def across(s, k, is_twin):
        @pl.when(is_twin)
        def _():
            low_copy(s, k).start()

        @pl.when(jnp.logical_not(is_twin))
        def _():
            x_copy(s, k, ACROSS).start()

    def own_sends(s):
        x_local(s).wait()
        x_copy(s, row, ACROSS).start()

        @pl.when(z + 1 < line)
        def _():
            x_copy(s, row, UP).start()

        @pl.when(z > 0)
        def _():
            x_copy(s, row, DOWN).start()

    def forward(s, d):
        @pl.when(z - d >= 0)
        def _():
            k = row - 2 * d
            x_copy(s, k, ACROSS).wait_recv()
            across(s, k, odd) if d == 1 else x_copy(s, k, ACROSS).start()

            @pl.when(z + 1 < line)
            def _():
                x_copy(s, k, UP).start()

        @pl.when(z + d < line)
        def _():
            k = row + 2 * d
            x_copy(s, k, ACROSS).wait_recv()
            across(s, k, jnp.logical_not(odd)) if d == 1 else x_copy(s, k, ACROSS).start()

            @pl.when(z > 0)
            def _():
                x_copy(s, k, DOWN).start()

    def uv_copy(which, d, slot):
        ref = (ug, vg)[which]
        return pltpu.make_async_remote_copy(
            src_ref=ref.at[slot], dst_ref=ref.at[slot],
            send_sem=uv_send.at[which, d], recv_sem=uv_recv.at[which, d],
            device_id=(row, lax.rem(col + d, n_col)), device_id_type=MESH,
        )

    own_sends(0)
    u_local.wait()
    v_local.wait()
    for d in range(1, n_col):
        uv_copy(0, d, col).start()
        uv_copy(1, d, col).start()
    for s in range(1, ahead):
        own_sends(s)

    q_local.wait()

    def turn_tiles(n):
        tiles = t_rows * t_cols

        @pl.loop(n * tiles // line, (n + 1) * tiles // line)
        def _(k):
            i, j = k // t_cols, lax.rem(k, t_cols)
            keep = lax.broadcasted_iota(jnp.int32, (rank_cap, u_rows), 0) < tile_rank[i, j]
            for b in range(order // u_rows):
                at = pl.ds(b * u_rows, u_rows)
                qt[i, j, :, at] = jnp.where(keep, qv[i, j, at, :].T, jnp.zeros((), BF16))

    turn_tiles(0)
    p_local.wait()
    def turn_panel():
        for d in range(1, n_col):
            slot = lax.rem(col + n_col - d, n_col)
            uv_copy(0, d, slot).wait_recv()
            uv_copy(1, d, slot).wait_recv()

        @pl.loop(0, t_rows)
        def _(i):
            keep = (
                lax.broadcasted_iota(jnp.int32, (rank_cap, u_rows), 0) < panel_rank[row * t_rows + i]
            )
            for b in range(n_col):
                at = pl.ds(b * u_rows, u_rows)
                ut[i, :, at] = jnp.where(keep, ug[b, i].T, jnp.zeros((), BF16))
                vt[i, :, at] = jnp.where(keep, vg[b, i].T, jnp.zeros((), BF16))

    def b_copy(s):
        return pltpu.make_async_remote_copy(
            src_ref=sbuf.at[s], dst_ref=rbuf.at[s],
            send_sem=b_send.at[s], recv_sem=b_recv.at[s],
            device_id=(row, owner(s)), device_id_type=MESH,
        )

    def sw_copy(s, k):
        return pltpu.make_async_remote_copy(
            src_ref=swb.at[s, k], dst_ref=swr.at[lax.rem(s, subs), row],
            send_sem=sw_send.at[s, k], recv_sem=sw_recv.at[lax.rem(s, subs), row],
            device_id=(k, owner(s)), device_id_type=MESH,
        )

    def compute(s):
        low_copy(s, twin + 1 - 2 * x).wait_recv()
        high_copy(s, twin + 1 - 2 * x).wait_recv()
        for e in range(1, line // 2):
            pair = lax.rem(z // 2 + e, line // 2)
            for b in range(2):
                x_copy(s, 2 * (2 * pair + b) + 1 - x, ACROSS).wait_recv()

        @pl.when(inside)
        def _():
            for i in range(t_rows):
                block = xg[s, :, first + i].reshape(order, width)
                proj = dot(ut[i], block).astype(BF16)
                term = dot(vg[:, i].reshape(order, rank_cap), proj)
                if i == 0:
                    sweep_acc[...] = term
                else:
                    sweep_acc[...] += term
            swb[s] = sweep_acc[...].astype(BF16).reshape(n_row, x_rows, width)

            @pl.loop(0, n_row)
            def _(k):
                mine = jnp.logical_and(k == row, s >= away)

                @pl.when(mine)
                def _():
                    swr[s - away, row] = swb[s, row]

                @pl.when(jnp.logical_not(mine))
                def _():
                    sw_copy(s, k).start()

        @pl.loop(0, t_rows)
        def _(i):
            total = None
            for j in range(t_cols):
                proj = dot(qt[i, j], xg[s, :, j].reshape(order, width)).astype(BF16)
                term = dot(pv[i, j], proj)
                total = term if total is None else total + term

            @pl.when(s < away)
            def _():
                sbuf[s, i] = total.astype(BF16)

            @pl.when(s >= away)
            def _():
                acc[lax.rem(s, subs), i] = total

        @pl.when(s < away)
        def _():
            b_copy(s).start()

    def reduce_sweep(h):
        for k in range(n_row):
            @pl.when(jnp.logical_not(jnp.logical_and(inside, k == row)))
            def _():
                pltpu.make_async_remote_copy(
                    src_ref=swr.at[h, k], dst_ref=swr.at[h, k],
                    send_sem=sw_send.at[h, k], recv_sem=sw_recv.at[h, k],
                    device_id=(row, col), device_id_type=MESH,
                ).wait_recv()

        total = swr[h, 0].astype(F32)
        for k in range(1, n_row):
            total = total + swr[h, k].astype(F32)
        swg[h, row] = total.astype(BF16)
        for e in range(1, line):
            g_along(h, e, row).start()
        g_across(h, 0, row).start()

    def g_along(h, e, slot):
        return pltpu.make_async_remote_copy(
            src_ref=swg.at[h, slot], dst_ref=swg.at[h, slot],
            send_sem=g_send.at[h, e], recv_sem=g_recv.at[h, slot],
            device_id=(2 * lax.rem(z + e, line) + x, col), device_id_type=MESH,
        )

    def g_across(h, e, slot):
        return pltpu.make_async_remote_copy(
            src_ref=swg.at[h, slot], dst_ref=swg.at[h, slot],
            send_sem=g_send.at[h, line + e], recv_sem=g_recv.at[h, slot],
            device_id=(mate, col), device_id_type=MESH,
        )

    def relay_sweep(h):
        for e in range(1, line):
            slot = 2 * lax.rem(z + line - e, line) + x
            g_along(h, e, slot).wait_recv()
            g_across(h, e, slot).start()

    def add_received(h):
        for g in range(n_col - 1):
            b_copy(g * subs + h).wait_recv()

        @pl.loop(0, t_rows)
        def _(i):
            total = acc[h, i]
            for g in range(n_col - 1):
                total = total + rbuf[g * subs + h, i].astype(F32)
            acc[h, i] = total

    def finish(h):
        for e in range(line):
            g_across(h, e, 2 * lax.rem(z + e, line) + 1 - x).wait_recv()

        @pl.loop(0, t_rows)
        def _(i):
            back = dot(vt[i], swg[h].reshape(order, width)).astype(BF16)
            late = dot(ug[:, i].reshape(order, rank_cap), back)
            out[i, :, h * width : (h + 1) * width] = (acc[h, i] - late).astype(BF16)

    @pl.loop(0, steps + 1)
    def _(s):
        @pl.when(s < steps)
        def _():
            forward(s, 1)
            x_copy(s, mate, ACROSS).wait_recv()
            high_copy(s, mate).start()

        @pl.when(s + ahead < steps)
        def _():
            own_sends(s + ahead)

        @pl.when(s == steps)
        def _():
            for h in range(subs - 1):
                reduce_sweep(h)

        for d in range(2, line):
            @pl.when(s == 0)
            def _():
                turn_tiles(d - 1)

            @pl.when(s < steps)
            def _():
                forward(s, d)

        @pl.when(s == 0)
        def _():
            turn_tiles(line - 1)

        @pl.when(s == 1)
        def _():
            turn_panel()

        @pl.when(s > 0)
        def _():
            compute(s - 1)

    reduce_sweep(subs - 1)
    for h in range(subs):
        add_received(h)
    for h in range(subs):
        relay_sweep(h)
    for h in range(subs):
        finish(h)

    @pl.loop(0, steps)
    def _(s):
        for m in range(line):
            k = 2 * m + x
            @pl.when(k == twin)
            def _():
                low_copy(s, k).wait_send()

            @pl.when(k != twin)
            def _():
                x_copy(s, k, ACROSS).wait_send()

            @pl.when(jnp.logical_and(m <= z, z + 1 < line))
            def _():
                x_copy(s, k, UP).wait_send()

            @pl.when(jnp.logical_and(m >= z, z > 0))
            def _():
                x_copy(s, k, DOWN).wait_send()

        high_copy(s, mate).wait_send()

        @pl.when(s < away)
        def _():
            b_copy(s).wait_send()

        @pl.when(inside)
        def _():
            @pl.loop(0, n_row)
            def _(k):
                @pl.when(jnp.logical_not(jnp.logical_and(k == row, s >= away)))
                def _():
                    sw_copy(s, k).wait_send()

    for d in range(1, n_col):
        uv_copy(0, d, col).wait_send()
        uv_copy(1, d, col).wait_send()
    for h in range(subs):
        for e in range(line):
            if e > 0:
                g_along(h, e, row).wait_send()
            g_across(h, e, row).wait_send()


def shards(n_row, n_col, x_rhs, panel_u, panel_v, panel_rank, tile_p, tile_q, tile_rank):
    t_rows, t_cols, order, rank_cap = tile_p.shape
    x_rows, n_rhs = x_rhs.shape[1:]
    u_rows = panel_u.shape[1]
    width = n_rhs // n_col
    subs = 1
    part = width // subs
    steps = n_col * subs
    away = steps - subs
    fits = (
        n_rhs % n_col == 0
        and width % (128 * subs) == 0
        and x_rows % 16 == 0
        and u_rows % 128 == 0
        and n_row % 4 == 0
        and n_col > 1
        and n_col & (n_col - 1) == 0
        and t_cols % t_rows == 0
        and t_cols % 2 == 0
    )
    if not fits:
        return plain(x_rhs, panel_u, panel_v, panel_rank, tile_p, tile_q, tile_rank)
    dma = pltpu.SemaphoreType.DMA
    flops = 4 * order * rank_cap * n_rhs * t_rows * (t_cols + 1)
    return pl.pallas_call(
        functools.partial(kernel, n_row, n_col),
        out_shape=jax.ShapeDtypeStruct((t_rows, order, width), BF16),
        in_specs=[pl.BlockSpec(memory_space=pltpu.SMEM)] * 2
        + [pl.BlockSpec(memory_space=pl.ANY)] * 5,
        out_specs=pl.BlockSpec(memory_space=pltpu.VMEM),
        scratch_shapes=[
            pltpu.VMEM((steps, n_row, t_cols, x_rows, part), BF16),
            pltpu.VMEM(tile_p.shape, BF16),
            pltpu.VMEM(tile_q.shape, BF16),
            pltpu.VMEM((t_rows, t_cols, rank_cap, order), BF16),
            pltpu.VMEM((n_col, t_rows, u_rows, rank_cap), BF16),
            pltpu.VMEM((n_col, t_rows, u_rows, rank_cap), BF16),
            pltpu.VMEM((t_rows, rank_cap, order), BF16),
            pltpu.VMEM((t_rows, rank_cap, order), BF16),
            pltpu.VMEM((subs, t_rows, order, part), F32),
            pltpu.VMEM((order, part), F32),
            pltpu.VMEM((away, t_rows, order, part), BF16),
            pltpu.VMEM((away, t_rows, order, part), BF16),
            pltpu.VMEM((steps, n_row, x_rows, part), BF16),
            pltpu.VMEM((subs, n_row, x_rows, part), BF16),
            pltpu.VMEM((subs, n_row, x_rows, part), BF16),
            dma((steps, n_row, 3)),
            dma((steps, n_row)),
            dma((steps,)),
            dma((steps,)),
            dma((2, n_col)),
            dma((2, n_col)),
            dma((away,)),
            dma((away,)),
            dma((steps, n_row)),
            dma((subs, n_row)),
            dma((subs, n_row)),
            dma((subs, n_row)),
            dma((steps + 4,)),
        ],
        compiler_params=pltpu.CompilerParams(
            collective_id=0, has_side_effects=True, vmem_limit_bytes=56 * 2**20
        ),
        cost_estimate=pl.CostEstimate(flops=flops, bytes_accessed=20 * 2**20, transcendentals=0),
    )(tile_rank, panel_rank, x_rhs, panel_u, panel_v, tile_p, tile_q)


def solution(mesh):
    return jax.shard_map(
        functools.partial(shards, mesh.shape["row"], mesh.shape["col"]),
        mesh=mesh,
        in_specs=(
            P("col", "row", None),
            P("row", "col", None),
            P("row", "col", None),
            P(),
            P("row", "col", None, None),
            P("row", "col", None, None),
            P("row", "col"),
        ),
        out_specs=P("row", None, "col"),
        check_vma=False,
    )
```

```python
import functools

import jax
import jax.numpy as jnp
from jax import lax
from jax.experimental import pallas as pl
from jax.experimental.pallas import tpu as pltpu
from jax.sharding import PartitionSpec as P

BF16 = jnp.bfloat16
F32 = jnp.float32
MESH = pl.DeviceIdType.MESH
UP, DOWN, ACROSS = 0, 1, 2


def plain(x_rhs, panel_u, panel_v, panel_rank, tile_p, tile_q, tile_rank):
    exact = lax.Precision.HIGHEST
    row_at = lax.axis_index("row")
    col_at = lax.axis_index("col")
    t_rows = tile_p.shape[0]
    t_cols = tile_p.shape[1]
    rank_cap = tile_p.shape[3]
    gathered = lax.all_gather(x_rhs, "row", axis=1, tiled=True)
    full_u, full_v = (
        lax.all_gather(panel_u, "col", axis=1, tiled=True),
        lax.all_gather(panel_v, "col", axis=1, tiled=True),
    )
    tile_slot = lax.broadcasted_iota(jnp.int32, (1, 1, rank_cap, 1), 2)
    tile_proj = jnp.einsum("ijbr,jbn->ijrn", tile_q, gathered, preferred_element_type=jnp.float32)
    tile_proj = jnp.where(tile_slot < tile_rank[:, :, None, None], tile_proj, 0.0).astype(
        jnp.bfloat16
    )
    base_sum = jnp.einsum("ijbr,ijrn->ibn", tile_p, tile_proj, preferred_element_type=jnp.float32)
    rank_slot = lax.broadcasted_iota(jnp.int32, (1, rank_cap, 1), 1)
    row_rank = lax.dynamic_slice_in_dim(panel_rank, row_at * t_rows, t_rows)
    row_keep = rank_slot < row_rank[:, None, None]
    u_wide = full_u.astype(jnp.float32)
    tile_ids = row_at * t_rows + jnp.arange(t_rows, dtype=jnp.int32)
    inside = tile_ids // t_cols == col_at
    where_rhs = jnp.clip(tile_ids - col_at * t_cols, 0, t_cols - 1)
    picked = jnp.take(gathered, where_rhs, axis=0)
    keep = jnp.logical_and(inside[:, None, None], row_keep)
    panel_proj = jnp.einsum("jbr,jbn->jrn", full_u, picked, preferred_element_type=jnp.float32)
    panel_proj = jnp.where(keep, panel_proj, 0.0).astype(jnp.bfloat16)
    sweep_part = jnp.einsum("jbr,jrn->bn", full_v, panel_proj, preferred_element_type=jnp.float32)
    sweep_share = lax.psum_scatter(
        sweep_part.astype(jnp.bfloat16), "col", scatter_dimension=1, tiled=True
    )
    sweep = lax.psum(sweep_share, "row").astype(jnp.float32)
    back_proj = jnp.einsum("ibr,bn->irn", full_v.astype(jnp.float32), sweep, precision=exact)
    back_proj = jnp.where(row_keep, back_proj, 0.0)
    late_term = jnp.einsum("ibr,irn->ibn", u_wide, back_proj, precision=exact)
    summed = lax.psum_scatter(
        base_sum.astype(jnp.bfloat16), "col", scatter_dimension=2, tiled=True
    ).astype(jnp.float32)
    return (summed - late_term).astype(jnp.bfloat16)


def dot(a, b):
    return jnp.dot(a, b, preferred_element_type=F32)


def kernel(
    n_row, n_col,
    tile_rank, panel_rank, x_in, u_in, v_in, p_in, q_in,
    out,
    xg, pv, qv, qt, ug, vg, ut, vt, acc, sweep_acc, sbuf, rbuf, swb, swr, swg,
    x_send, x_recv, h_send, h_recv, uv_send, uv_recv, b_send, b_recv, sw_send, sw_recv, g_send, g_recv, local,
):
    t_rows, t_cols, order, rank_cap = pv.shape
    x_rows = xg.shape[3]
    width = xg.shape[4]
    u_rows = ug.shape[2]
    subs = swr.shape[0]
    steps = n_col * subs
    away = steps - subs
    ahead = 2
    half = t_cols // 2
    line = n_row // 2
    row = lax.axis_index("row")
    col = lax.axis_index("col")
    z, x = row // 2, row % 2
    mate = row + 1 - 2 * x
    odd = z % 2 == 1
    twin = row + 2 - 4 * (z % 2)
    inside = (row * t_rows) // t_cols == col
    first = lax.rem(row * t_rows, t_cols)

    def owner(s):
        flip = n_col - 1 - s // subs
        bits = [1 << b for b in range(n_col.bit_length() - 1)]
        return sum(lax.rem(col // b + flip // b, 2) * b for b in bits)

    def x_local(s):
        at = pl.multiple_of((owner(s) * subs + lax.rem(s, subs)) * width, width)
        return pltpu.make_async_copy(x_in.at[:, :, pl.ds(at, width)], xg.at[s, row], local.at[s])

    q_local = pltpu.make_async_copy(q_in, qv, local.at[steps])
    p_local = pltpu.make_async_copy(p_in, pv, local.at[steps + 1])
    u_local = pltpu.make_async_copy(u_in, ug.at[col], local.at[steps + 2])
    v_local = pltpu.make_async_copy(v_in, vg.at[col], local.at[steps + 3])
    x_local(0).start()
    u_local.start()
    v_local.start()
    for s in range(1, steps):
        x_local(s).start()
    q_local.start()
    p_local.start()

    barrier = pltpu.get_barrier_semaphore()

    @pl.loop(0, n_row * n_col)
    def _(k):
        @pl.when(k != row * n_col + col)
        def _():
            pl.semaphore_signal(
                barrier, inc=1, device_id=(k // n_col, lax.rem(k, n_col)), device_id_type=MESH
            )

    pl.semaphore_wait(barrier, n_row * n_col - 1)

    def x_copy(s, k, way):
        target = {UP: row + 2, DOWN: row - 2, ACROSS: mate}[way]
        return pltpu.make_async_remote_copy(
            src_ref=xg.at[s, k], dst_ref=xg.at[s, k],
            send_sem=x_send.at[s, k, way], recv_sem=x_recv.at[s, k],
            device_id=(target, col), device_id_type=MESH,
        )

    def low_copy(s, k):
        return pltpu.make_async_remote_copy(
            src_ref=xg.at[s, k, :half], dst_ref=xg.at[s, k, :half],
            send_sem=x_send.at[s, k, ACROSS], recv_sem=x_recv.at[s, k],
            device_id=(mate, col), device_id_type=MESH,
        )

    def high_copy(s, k):
        return pltpu.make_async_remote_copy(
            src_ref=xg.at[s, k, half:], dst_ref=xg.at[s, k, half:],
            send_sem=h_send.at[s], recv_sem=h_recv.at[s],
            device_id=(twin, col), device_id_type=MESH,
        )

    def across(s, k, is_twin):
        @pl.when(is_twin)
        def _():
            low_copy(s, k).start()

        @pl.when(jnp.logical_not(is_twin))
        def _():
            x_copy(s, k, ACROSS).start()

    def own_sends(s):
        x_local(s).wait()
        x_copy(s, row, ACROSS).start()

        @pl.when(z + 1 < line)
        def _():
            x_copy(s, row, UP).start()

        @pl.when(z > 0)
        def _():
            x_copy(s, row, DOWN).start()

    def forward(s, d):
        @pl.when(z - d >= 0)
        def _():
            k = row - 2 * d
            x_copy(s, k, ACROSS).wait_recv()
            across(s, k, odd) if d == 1 else x_copy(s, k, ACROSS).start()

            @pl.when(z + 1 < line)
            def _():
                x_copy(s, k, UP).start()

        @pl.when(z + d < line)
        def _():
            k = row + 2 * d
            x_copy(s, k, ACROSS).wait_recv()
            across(s, k, jnp.logical_not(odd)) if d == 1 else x_copy(s, k, ACROSS).start()

            @pl.when(z > 0)
            def _():
                x_copy(s, k, DOWN).start()

    def uv_copy(which, d, slot):
        ref = (ug, vg)[which]
        return pltpu.make_async_remote_copy(
            src_ref=ref.at[slot], dst_ref=ref.at[slot],
            send_sem=uv_send.at[which, d], recv_sem=uv_recv.at[which, d],
            device_id=(row, lax.rem(col + d, n_col)), device_id_type=MESH,
        )

    own_sends(0)
    u_local.wait()
    v_local.wait()
    for d in range(1, n_col):
        uv_copy(0, d, col).start()
        uv_copy(1, d, col).start()
    for s in range(1, ahead):
        own_sends(s)

    q_local.wait()

    @pl.loop(0, t_rows * t_cols)
    def _(k):
        i, j = k // t_cols, lax.rem(k, t_cols)
        keep = lax.broadcasted_iota(jnp.int32, (rank_cap, u_rows), 0) < tile_rank[i, j]
        for b in range(order // u_rows):
            at = pl.ds(b * u_rows, u_rows)
            qt[i, j, :, at] = jnp.where(keep, qv[i, j, at, :].T, jnp.zeros((), BF16))

    p_local.wait()
    for d in range(1, n_col):
        slot = lax.rem(col + n_col - d, n_col)
        uv_copy(0, d, slot).wait_recv()
        uv_copy(1, d, slot).wait_recv()

    @pl.loop(0, t_rows)
    def _(i):
        keep = (
            lax.broadcasted_iota(jnp.int32, (rank_cap, u_rows), 0) < panel_rank[row * t_rows + i]
        )
        for b in range(n_col):
            at = pl.ds(b * u_rows, u_rows)
            ut[i, :, at] = jnp.where(keep, ug[b, i].T, jnp.zeros((), BF16))
            vt[i, :, at] = jnp.where(keep, vg[b, i].T, jnp.zeros((), BF16))

    def b_copy(s):
        return pltpu.make_async_remote_copy(
            src_ref=sbuf.at[s], dst_ref=rbuf.at[s],
            send_sem=b_send.at[s], recv_sem=b_recv.at[s],
            device_id=(row, owner(s)), device_id_type=MESH,
        )

    def sw_copy(s, k):
        return pltpu.make_async_remote_copy(
            src_ref=swb.at[s, k], dst_ref=swr.at[lax.rem(s, subs), row],
            send_sem=sw_send.at[s, k], recv_sem=sw_recv.at[lax.rem(s, subs), row],
            device_id=(k, owner(s)), device_id_type=MESH,
        )

    def sweep_terms(s):
        low_copy(s, twin + 1 - 2 * x).wait_recv()
        high_copy(s, twin + 1 - 2 * x).wait_recv()
        for e in range(1, line // 2):
            pair = lax.rem(z // 2 + e, line // 2)
            for b in range(2):
                x_copy(s, 2 * (2 * pair + b) + 1 - x, ACROSS).wait_recv()

        @pl.when(inside)
        def _():
            for i in range(t_rows):
                block = xg[s, :, first + i].reshape(order, width)
                proj = dot(ut[i], block).astype(BF16)
                term = dot(vg[:, i].reshape(order, rank_cap), proj)
                if i == 0:
                    sweep_acc[...] = term
                else:
                    sweep_acc[...] += term
            swb[s] = sweep_acc[...].astype(BF16).reshape(n_row, x_rows, width)

            @pl.loop(0, n_row)
            def _(k):
                mine = jnp.logical_and(k == row, s >= away)

                @pl.when(mine)
                def _():
                    swr[s - away, row] = swb[s, row]

                @pl.when(jnp.logical_not(mine))
                def _():
                    sw_copy(s, k).start()

    def base_rows(s, lo, hi):
        @pl.loop(lo, hi)
        def _(i):
            total = None
            for j in range(t_cols):
                proj = dot(qt[i, j], xg[s, :, j].reshape(order, width)).astype(BF16)
                term = dot(pv[i, j], proj)
                total = term if total is None else total + term

            @pl.when(s < away)
            def _():
                sbuf[s, i] = total.astype(BF16)

            @pl.when(s >= away)
            def _():
                acc[lax.rem(s, subs), i] = total

        if lo == 0 and hi == t_rows:
            b_copy(s).start()

    def reduce_sweep(h):
        for k in range(n_row):
            @pl.when(jnp.logical_not(jnp.logical_and(inside, k == row)))
            def _():
                pltpu.make_async_remote_copy(
                    src_ref=swr.at[h, k], dst_ref=swr.at[h, k],
                    send_sem=sw_send.at[h, k], recv_sem=sw_recv.at[h, k],
                    device_id=(row, col), device_id_type=MESH,
                ).wait_recv()

        total = swr[h, 0].astype(F32)
        for k in range(1, n_row):
            total = total + swr[h, k].astype(F32)
        swg[h, row] = total.astype(BF16)
        for e in range(1, line):
            g_along(h, e, row).start()
        g_across(h, 0, row).start()

    def g_along(h, e, slot):
        return pltpu.make_async_remote_copy(
            src_ref=swg.at[h, slot], dst_ref=swg.at[h, slot],
            send_sem=g_send.at[h, e], recv_sem=g_recv.at[h, slot],
            device_id=(2 * lax.rem(z + e, line) + x, col), device_id_type=MESH,
        )

    def g_across(h, e, slot):
        return pltpu.make_async_remote_copy(
            src_ref=swg.at[h, slot], dst_ref=swg.at[h, slot],
            send_sem=g_send.at[h, line + e], recv_sem=g_recv.at[h, slot],
            device_id=(mate, col), device_id_type=MESH,
        )

    def relay_sweep(h):
        for e in range(1, line):
            slot = 2 * lax.rem(z + line - e, line) + x
            g_along(h, e, slot).wait_recv()
            g_across(h, e, slot).start()

    def add_received(h):
        for g in range(n_col - 1):
            b_copy(g * subs + h).wait_recv()

        @pl.loop(0, t_rows)
        def _(i):
            total = acc[h, i]
            for g in range(n_col - 1):
                total = total + rbuf[g * subs + h, i].astype(F32)
            acc[h, i] = total

    def finish(h):
        for e in range(line):
            g_across(h, e, 2 * lax.rem(z + e, line) + 1 - x).wait_recv()

        @pl.loop(0, t_rows)
        def _(i):
            back = dot(vt[i], swg[h].reshape(order, width)).astype(BF16)
            late = dot(ug[:, i].reshape(order, rank_cap), back)
            out[i, :, h * width : (h + 1) * width] = (acc[h, i] - late).astype(BF16)

    @pl.loop(0, steps)
    def _(s):
        @pl.when(s < steps)
        def _():
            forward(s, 1)
            x_copy(s, mate, ACROSS).wait_recv()
            high_copy(s, mate).start()

        @pl.when(s + ahead < steps)
        def _():
            own_sends(s + ahead)

        @pl.when(s < steps)
        def _():
            for d in range(2, line):
                forward(s, d)

        @pl.when(s > 0)
        def _():
            sweep_terms(s - 1)
            base_rows(s - 1, 0, t_rows)

    last = jnp.int32(steps - 1)
    sweep_terms(last)
    base_rows(last, 0, t_rows // 2)
    reduce_sweep(0)
    base_rows(last, t_rows // 2, t_rows)
    for h in range(subs):
        relay_sweep(h)
    for h in range(subs):
        add_received(h)
        finish(h)

    @pl.loop(0, steps)
    def _(s):
        for m in range(line):
            k = 2 * m + x
            @pl.when(k == twin)
            def _():
                low_copy(s, k).wait_send()

            @pl.when(k != twin)
            def _():
                x_copy(s, k, ACROSS).wait_send()

            @pl.when(jnp.logical_and(m <= z, z + 1 < line))
            def _():
                x_copy(s, k, UP).wait_send()

            @pl.when(jnp.logical_and(m >= z, z > 0))
            def _():
                x_copy(s, k, DOWN).wait_send()

        high_copy(s, mate).wait_send()

        @pl.when(s < away)
        def _():
            b_copy(s).wait_send()

        @pl.when(inside)
        def _():
            @pl.loop(0, n_row)
            def _(k):
                @pl.when(jnp.logical_not(jnp.logical_and(k == row, s >= away)))
                def _():
                    sw_copy(s, k).wait_send()

    for d in range(1, n_col):
        uv_copy(0, d, col).wait_send()
        uv_copy(1, d, col).wait_send()
    for h in range(subs):
        for e in range(line):
            if e > 0:
                g_along(h, e, row).wait_send()
            g_across(h, e, row).wait_send()


def shards(n_row, n_col, x_rhs, panel_u, panel_v, panel_rank, tile_p, tile_q, tile_rank):
    t_rows, t_cols, order, rank_cap = tile_p.shape
    x_rows, n_rhs = x_rhs.shape[1:]
    u_rows = panel_u.shape[1]
    width = n_rhs // n_col
    subs = 1
    part = width // subs
    steps = n_col * subs
    away = steps - subs
    fits = (
        n_rhs % n_col == 0
        and width % (128 * subs) == 0
        and x_rows % 16 == 0
        and u_rows % 128 == 0
        and n_row % 4 == 0
        and n_col > 1
        and n_col & (n_col - 1) == 0
        and t_rows > 1
        and t_cols % t_rows == 0
        and t_cols % 2 == 0
    )
    if not fits:
        return plain(x_rhs, panel_u, panel_v, panel_rank, tile_p, tile_q, tile_rank)
    dma = pltpu.SemaphoreType.DMA
    flops = 4 * order * rank_cap * n_rhs * t_rows * (t_cols + 1)
    return pl.pallas_call(
        functools.partial(kernel, n_row, n_col),
        out_shape=jax.ShapeDtypeStruct((t_rows, order, width), BF16),
        in_specs=[pl.BlockSpec(memory_space=pltpu.SMEM)] * 2
        + [pl.BlockSpec(memory_space=pl.ANY)] * 5,
        out_specs=pl.BlockSpec(memory_space=pltpu.VMEM),
        scratch_shapes=[
            pltpu.VMEM((steps, n_row, t_cols, x_rows, part), BF16),
            pltpu.VMEM(tile_p.shape, BF16),
            pltpu.VMEM(tile_q.shape, BF16),
            pltpu.VMEM((t_rows, t_cols, rank_cap, order), BF16),
            pltpu.VMEM((n_col, t_rows, u_rows, rank_cap), BF16),
            pltpu.VMEM((n_col, t_rows, u_rows, rank_cap), BF16),
            pltpu.VMEM((t_rows, rank_cap, order), BF16),
            pltpu.VMEM((t_rows, rank_cap, order), BF16),
            pltpu.VMEM((subs, t_rows, order, part), F32),
            pltpu.VMEM((order, part), F32),
            pltpu.VMEM((away, t_rows, order, part), BF16),
            pltpu.VMEM((away, t_rows, order, part), BF16),
            pltpu.VMEM((steps, n_row, x_rows, part), BF16),
            pltpu.VMEM((subs, n_row, x_rows, part), BF16),
            pltpu.VMEM((subs, n_row, x_rows, part), BF16),
            dma((steps, n_row, 3)),
            dma((steps, n_row)),
            dma((steps,)),
            dma((steps,)),
            dma((2, n_col)),
            dma((2, n_col)),
            dma((away,)),
            dma((away,)),
            dma((steps, n_row)),
            dma((subs, n_row)),
            dma((subs, n_row)),
            dma((subs, n_row)),
            dma((steps + 4,)),
        ],
        compiler_params=pltpu.CompilerParams(
            collective_id=0, has_side_effects=True, vmem_limit_bytes=56 * 2**20
        ),
        cost_estimate=pl.CostEstimate(flops=flops, bytes_accessed=20 * 2**20, transcendentals=0),
    )(tile_rank, panel_rank, x_rhs, panel_u, panel_v, tile_p, tile_q)


def solution(mesh):
    return jax.shard_map(
        functools.partial(shards, mesh.shape["row"], mesh.shape["col"]),
        mesh=mesh,
        in_specs=(
            P("col", "row", None),
            P("row", "col", None),
            P("row", "col", None),
            P(),
            P("row", "col", None, None),
            P("row", "col", None, None),
            P("row", "col"),
        ),
        out_specs=P("row", None, "col"),
        check_vma=False,
    )
```
